512 devices in a mesh: expert: 64 (over x, y, z_hi), fsdp: 8 (over z_lo, core).
Axes of the slice: x: 4, y: 4, z: 16 (z_hi: 4, z_lo: 4; z = z_hi * 4 + z_lo), core: 2. Of those that a mesh axis runs over, the one named last changes fastest.
Arguments:
- tokens: bfloat16 [8192, 4096], P('expert', 'fsdp'), may hold values from -6 to 6
- routes: int32 [8192, 8], P('expert'), may hold values from 0 to 63, all different within a row; in each aligned block of 128 rows (0 to 127, 128 to 255, ...) at most 32 rows name the same one
- hidden_grad: bfloat16 [8192, 8, 768], P('expert', None, 'fsdp'), may hold values from -6 to 6
- gate_base: bfloat16 [4096, 768], P('fsdp'), may hold values from -0.09375 to 0.09375
- up_base: bfloat16 [4096, 768], P('fsdp'), may hold values from -0.09375 to 0.09375
- gate_left: bfloat16 [64, 4096, 128], P('expert', 'fsdp'), may hold values from -0.09375 to 0.09375
- up_left: bfloat16 [64, 4096, 128], P('expert', 'fsdp'), may hold values from -0.09375 to 0.09375
- gate_right: bfloat16 [64, 128, 768], P('expert', None, 'fsdp'), may hold values from -0.5 to 0.5
- up_right: bfloat16 [64, 128, 768], P('expert', None, 'fsdp'), may hold values from -0.5 to 0.5
Outputs:
- tokens_grad: bfloat16 [8192, 4096], P('expert', 'fsdp')
- gate_base_grad: float32 [4096, 768], P(('fsdp', 'expert'))
- up_base_grad: float32 [4096, 768], P(('fsdp', 'expert'))
- gate_left_grad: float32 [64, 4096, 128], P('expert', 'fsdp')
- up_left_grad: float32 [64, 4096, 128], P('expert', 'fsdp')
- gate_right_grad: float32 [64, 128, 768], P('expert', None, 'fsdp')
- up_right_grad: float32 [64, 128, 768], P('expert', None, 'fsdp')
The draws below stay inside these ranges and needn't reach their ends.
Inputs may be any that keep to these rules, and one draw needn't show every extreme that they name: `routes`: each row names 8 different experts. Within the tokens of one index of expert, no expert is named more than 32 times, a bound that some block reaches.
All inputs are finite; a program needn't handle non-finite values.
Results may differ from the reference program's by a relative error of at most 0.0069.
Values may be sent and summed in bfloat16 or wider, within the bound.
A program may use at most 64 MiB of HBM per device.

```python
import math
import jax
import jax.numpy as jnp
import numpy as np
from jax import lax

D = 4096
FF = 768
R = 128
TOPK = 8
TOK_DEV = 128
EXPERTS = 64
TOKENS = 8192
CAP = 32


def shard_levels(stream_key, dims, pieces, least, largest):
    def one(dim, shards_of):
        heights = jax.random.uniform(jax.random.fold_in(jax.random.fold_in(stream_key, 6), dim), (shards_of,), jnp.float32, least / len(pieces), largest / len(pieces))
        return jnp.repeat(jnp.exp(heights), dims[dim] // shards_of).reshape((-1,) + (1,) * (len(dims) - dim - 1))

    gain = one(*pieces[0])
    for cut in pieces[1:]:
        gain = gain * one(*cut)
    return gain


def assign_block(key, own, number, rows, number_of, top, most, lean):
    order = jax.random.permutation(key, number_of)
    packed, common = portions_of(number_of, rows * top, most, lean, True), portions_of(number_of, rows * top, most, lean, False)
    places = jnp.arange(number_of)

    def named(sizes, turn):
        used = int((sizes > 0).sum())
        fixed = max(1, used // 4)
        shifted = fixed + (places - fixed + turn * (used - fixed)) % max(1, number_of - fixed)
        return jnp.zeros((number_of,), jnp.int32).at[order[jnp.where(places < fixed, places, shifted)]].set(jnp.asarray(sizes, jnp.int32))

    sizes = jnp.where(number % 4 == 0, named(packed, number // 4), named(common, number - number // 4 - 1))
    mixed = jax.random.permutation(jax.random.fold_in(own, 3), number_of)
    donor, receiver = mixed[0:number_of // 2 * 2:2], mixed[1:number_of // 2 * 2:2]
    room = jnp.minimum(sizes[donor] - 1, most - sizes[receiver]) // 2
    room = jnp.where((donor == order[0]) | (receiver == order[0]) | (sizes[receiver] == 0), 0, jnp.maximum(room, 0))
    shifted = jax.random.randint(jax.random.fold_in(own, 4), (number_of // 2,), 0, 1 << 20) % (room + 1)
    sizes = sizes.at[donor].add(-shifted).at[receiver].add(shifted)
    items = jnp.searchsorted(jnp.cumsum(sizes), jnp.arange(rows * top), side="right").astype(jnp.int32)
    grid = items.reshape(top, rows).T
    grid = grid[jax.random.permutation(jax.random.fold_in(own, 1), rows)]
    turn = jax.random.randint(jax.random.fold_in(own, 2), (rows, 1), 0, top)
    return jnp.take_along_axis(grid, (jnp.arange(top)[None, :] + turn) % top, axis=1)


def portions_of(amount, total, bound, slope, full):
    weights = [(1 << 20) // math.isqrt(standing ** slope) + 1 for standing in range(1, amount + 1)]
    largest = bound if full else min(bound, max(-(-total // amount), total * weights[0] // sum(weights)))
    least = 1 if total - largest >= amount - 1 else 0
    counts, spare = [largest] + [least] * (amount - 1), total - largest - least * (amount - 1)
    while spare > 0:
        free = [i for i in range(1, amount) if counts[i] < largest] or [i for i in range(1, amount) if counts[i] < bound]
        mass, left = sum([weights[i] for i in free]), spare
        for i in free:
            addition = min(bound - counts[i], max(1, left * weights[i] // mass), spare)
            counts[i] = counts[i] + addition
            spare = spare - addition
    return np.array(counts)


def scatter_about(stream_key, shape, deviation, reach, shards=(), kind=jnp.bfloat16):
    level = shard_levels(stream_key, shape, shards, -0.22, 0.18) if shards else 1.0
    drawn = jax.random.normal(stream_key, shape, jnp.float32) * deviation * level
    return jnp.minimum(jnp.maximum(drawn, -reach), reach).astype(kind)


def setup_inputs(seed: int = 0) -> dict:
    arg_keys = jax.random.split(jax.random.key(seed), 10)
    tokens = scatter_about(arg_keys[0], (TOKENS, D), 1.0, 6.0, ((0, 64), (1, 8)))
    routes_keys = jax.random.split(jax.random.fold_in(arg_keys[1], 1), TOKENS // TOK_DEV)
    routes_turns = jax.random.permutation(jax.random.fold_in(arg_keys[1], 3), TOKENS // TOK_DEV)
    routes = jax.vmap(lambda own, number: assign_block(jax.random.fold_in(arg_keys[1], 2), own, number, TOK_DEV, EXPERTS, TOPK, CAP, 2))(routes_keys, routes_turns).reshape((TOKENS, TOPK))
    hidden_grad = scatter_about(arg_keys[2], (TOKENS, TOPK, FF), 1.0, 6.0, ((0, 64), (2, 8)))
    gate_base = scatter_about(arg_keys[3], (D, FF), D ** -0.5, 0.09375, ((0, 8),))
    up_base = scatter_about(arg_keys[4], (D, FF), D ** -0.5, 0.09375, ((0, 8),))
    gate_left = scatter_about(arg_keys[5], (EXPERTS, D, R), D ** -0.5, 0.09375, ((0, 64), (1, 8)))
    up_left = scatter_about(arg_keys[6], (EXPERTS, D, R), D ** -0.5, 0.09375, ((0, 64), (1, 8)))
    gate_right = scatter_about(arg_keys[7], (EXPERTS, R, FF), R ** -0.5, 0.5, ((0, 64), (2, 8)))
    up_right = scatter_about(arg_keys[8], (EXPERTS, R, FF), R ** -0.5, 0.5, ((0, 64), (2, 8)))
    return dict(tokens=tokens, routes=routes, hidden_grad=hidden_grad, gate_base=gate_base, up_base=up_base, gate_left=gate_left, up_left=up_left, gate_right=gate_right, up_right=up_right)


def slot_owner(routes):
    blocks = routes.shape[0] // TOK_DEV
    per_block = TOK_DEV * TOPK
    table = routes.reshape(blocks, per_block)
    onehot_table = (table[:, :, None] == jnp.arange(EXPERTS, dtype=jnp.int32)[None, None, :]).astype(jnp.int32)
    earlier = jnp.cumsum(onehot_table, axis=1) - onehot_table
    place = jnp.sum(earlier * onehot_table, axis=2).astype(jnp.int32)
    block_ids = jnp.arange(blocks, dtype=jnp.int32)[:, None]
    flat_slot = (table * blocks + block_ids) * CAP + place
    copy_ids = block_ids * per_block + jnp.arange(per_block, dtype=jnp.int32)[None, :]
    owner = jnp.full((EXPERTS * blocks * CAP,), -1, jnp.int32).at[flat_slot.reshape(-1)].set(copy_ids.reshape(-1))
    return owner.reshape(EXPERTS, blocks * CAP)


def reference(tokens, routes, hidden_grad, gate_base, up_base, gate_left, up_left, gate_right, up_right):
    gate_act = jnp.dot(tokens, gate_base, preferred_element_type=jnp.float32).astype(jnp.bfloat16)
    up_act = jnp.dot(tokens, up_base, preferred_element_type=jnp.float32).astype(jnp.bfloat16)
    owner = slot_owner(routes)
    hidden_flat = hidden_grad.reshape(TOKENS * TOPK, FF)

    def per_expert(carry, expert_id):
        acc_dx, acc_gate, acc_up = carry
        own = owner[expert_id]
        filled = (own >= 0)[:, None]
        safe_copy = jnp.where(own >= 0, own, 0)
        safe_token = safe_copy // TOPK
        x_rows = jnp.where(filled, tokens[safe_token], jnp.zeros((), jnp.bfloat16))
        gate_rows = jnp.where(filled, gate_act[safe_token], jnp.zeros((), jnp.bfloat16))
        up_rows = jnp.where(filled, up_act[safe_token], jnp.zeros((), jnp.bfloat16))
        hidden_rows = jnp.where(filled, hidden_flat[safe_copy], jnp.zeros((), jnp.bfloat16))
        gate_low = jnp.dot(x_rows, gate_left[expert_id], preferred_element_type=jnp.float32).astype(jnp.bfloat16)
        up_low = jnp.dot(x_rows, up_left[expert_id], preferred_element_type=jnp.float32).astype(jnp.bfloat16)
        gate_pre = gate_rows.astype(jnp.float32) + jnp.dot(gate_low, gate_right[expert_id], preferred_element_type=jnp.float32)
        up_pre = up_rows.astype(jnp.float32) + jnp.dot(up_low, up_right[expert_id], preferred_element_type=jnp.float32)
        sigma = jax.nn.sigmoid(gate_pre)
        hidden_f = hidden_rows.astype(jnp.float32)
        d_gate = (hidden_f * up_pre * sigma * (1.0 + gate_pre * (1.0 - sigma))).astype(jnp.bfloat16)
        d_up = (hidden_f * gate_pre * sigma).astype(jnp.bfloat16)
        gate_right_g = jnp.dot(gate_low.T, d_gate, preferred_element_type=jnp.float32)
        up_right_g = jnp.dot(up_low.T, d_up, preferred_element_type=jnp.float32)
        d_gate_low = jnp.dot(d_gate, gate_right[expert_id].T, preferred_element_type=jnp.float32).astype(jnp.bfloat16)
        d_up_low = jnp.dot(d_up, up_right[expert_id].T, preferred_element_type=jnp.float32).astype(jnp.bfloat16)
        gate_left_g = jnp.dot(x_rows.T, d_gate_low, preferred_element_type=jnp.float32)
        up_left_g = jnp.dot(x_rows.T, d_up_low, preferred_element_type=jnp.float32)
        delta_dx = (jnp.dot(d_gate_low, gate_left[expert_id].T, preferred_element_type=jnp.float32)
                    + jnp.dot(d_up_low, up_left[expert_id].T, preferred_element_type=jnp.float32)).astype(jnp.bfloat16)
        zero_f = jnp.zeros((), jnp.float32)
        acc_dx = acc_dx.at[safe_token].add(jnp.where(filled, delta_dx.astype(jnp.float32), zero_f))
        acc_gate = acc_gate.at[safe_token].add(jnp.where(filled, d_gate.astype(jnp.float32), zero_f))
        acc_up = acc_up.at[safe_token].add(jnp.where(filled, d_up.astype(jnp.float32), zero_f))
        return (acc_dx, acc_gate, acc_up), (gate_left_g, up_left_g, gate_right_g, up_right_g)

    start = (jnp.zeros((TOKENS, D), jnp.float32), jnp.zeros((TOKENS, FF), jnp.float32), jnp.zeros((TOKENS, FF), jnp.float32))
    (acc_dx, acc_gate, acc_up), stacked = lax.scan(per_expert, start, jnp.arange(EXPERTS, dtype=jnp.int32))
    gate_sum = acc_gate.astype(jnp.bfloat16)
    up_sum = acc_up.astype(jnp.bfloat16)
    gate_base_grad = jnp.dot(tokens.T, gate_sum, preferred_element_type=jnp.float32)
    up_base_grad = jnp.dot(tokens.T, up_sum, preferred_element_type=jnp.float32)
    tokens_grad = (acc_dx + jnp.dot(gate_sum, gate_base.T, preferred_element_type=jnp.float32)
                   + jnp.dot(up_sum, up_base.T, preferred_element_type=jnp.float32)).astype(jnp.bfloat16)
    return (tokens_grad, gate_base_grad, up_base_grad, stacked[0], stacked[1], stacked[2], stacked[3])
```

```python
import jax
import jax.numpy as jnp
from jax import lax
from jax.experimental import pallas as pl
from jax.experimental.pallas import tpu as pltpu
from jax.sharding import PartitionSpec as P

BF = jnp.bfloat16
F32 = jnp.float32
MESH = pl.DeviceIdType.MESH
TOK = 128
FEAT = 512
HID = 96
FF = 768
R = 128
CAP = 32
XROWS = 528
WROWS = 1216
SEMS = 288


def dot(a, b, ca=1, cb=0):
    return lax.dot_general(a, b, (((ca,), (cb,)), ((), ())), preferred_element_type=F32)


def iota(shape, dim):
    return lax.broadcasted_iota(jnp.int32, shape, dim)


SCRATCH = dict(
    xb=((4, 4, XROWS, TOK), BF),
    wb=((4, WROWS, R), BF),
    lt=((4, 2 * R, FEAT), BF),
    ap=((4, 2, 2 * HID, TOK), BF),
    ac=((4, 2 * HID, TOK), BF),
    as_=((4, 2 * HID, TOK), BF),
    az=((3, 2 * HID, TOK), BF),
    ab=((4, 4, 2 * HID, TOK), BF),
    ho=((4, 4, HID, TOK), BF),
    hm=((4, 4, HID, TOK), BF),
    hb=((4, 4, HID, TOK), BF),
    pm=((4 * TOK, 4 * TOK), BF),
    pb=((4, 4 * TOK, 4 * TOK), BF),
    xs=((4, FEAT, 4 * TOK), BF),
    lp=((4, 2, 4, R, TOK), BF),
    lc=((4, 4, R, TOK), BF),
    ls=((4, 4, R, TOK), BF),
    lz=((4, 3, R, TOK), BF),
    lo=((4, 2, 4, R, TOK), BF),
    kp=((4, 2, 4, R, TOK), BF),
    kc=((4, 4, R, TOK), BF),
    ks=((4, 4, R, TOK), BF),
    kz=((4, 3, R, TOK), BF),
    ko=((4, 2, 4, R, TOK), BF),
    dg=((4, 2 * HID, 4 * TOK), BF),
    gp=((4, 4, 2 * HID, TOK), BF),
    gr=((4, 2, HID, TOK), BF),
    gf=((4, 2, 2 * HID, TOK), BF),
    gq=((4, 2 * HID, TOK), BF),
    hr=((2, HID, TOK), BF),
    hf=((2, 2 * HID, TOK), BF),
    gs=((2, 4, 2, HID, TOK), BF),
    dp=((4, 4, FEAT, TOK), BF),
    dr=((4, 2, FEAT // 2, TOK), BF),
    df=((4, 2, FEAT, TOK), BF),
    dq=((4, FEAT, TOK), BF),
    er=((2, FEAT // 2, TOK), BF),
    ef=((2, FEAT, TOK), BF),
    wg=((4, WROWS, R), BF),
    wr=((2, WROWS // 2, R), BF),
    wf=((2, WROWS, R), BF),
    bg=((4, 4, 4, 16, FF), BF),
    bxr=((2, 2, 4, 16, FF), BF),
    bxf=((2, 4, 4, 16, FF), BF),
    by=((4, 4, 16, FF), BF),
    byr=((2, 2, 16, FF), BF),
    byf=((2, 4, 16, FF), BF),
    bz=((4, 16, FF), BF),
    bzr=((2, 16, FF // 2), BF),
    bzf=((2, 16, FF), BF),
)


def kernel(*refs):
    (tokens, routes, hidden, gbase, ubase, gleft, uleft, gright, uright) = refs[:9]
    (o_tok, o_gb, o_ub, o_gl, o_ul, o_gr, o_ur) = refs[9:16]
    s = dict(zip(SCRATCH, refs[16 : 16 + len(SCRATCH)]))
    send_sem, recv_sem = refs[16 + len(SCRATCH) :]

    e = lax.axis_index("expert")
    f = lax.axis_index("fsdp")
    x, y, h = e // 16, (e // 4) % 4, e % 4
    l, c = f // 2, f % 2

    def at(dx=0, dy=0, dh=0, dl=0, dc=0):
        return (
            ((x + dx) % 4) * 16 + ((y + dy) % 4) * 4 + (h + dh) % 4,
            ((l + dl) % 4) * 2 + (c + dc) % 2,
        )

    peers = [dict(dx=1), dict(dx=3), dict(dy=1), dict(dy=2), dict(dy=3), dict(dh=1), dict(dh=2), dict(dh=3)]
    peers += [dict(dl=1), dict(dl=2), dict(dl=3), dict(dc=1)]
    barrier = pltpu.get_barrier_semaphore()
    for peer in peers:
        pl.semaphore_signal(barrier, inc=1, device_id=at(**peer), device_id_type=MESH)
    pl.semaphore_wait(barrier, len(peers))

    started = []

    def send(src, dst, **where):
        n = len(started)
        copy = pltpu.make_async_remote_copy(
            src_ref=src,
            dst_ref=dst,
            send_sem=send_sem.at[n],
            recv_sem=recv_sem.at[n],
            device_id=at(**where),
            device_id_type=MESH,
        )
        copy.start()
        started.append(copy)
        return copy

    class Gather:
        def __init__(self, axis, buf, first, second):
            self.axis, self.buf, self.first, self.second = axis, buf, first, second

        def start(self):
            self.right = send(self.buf(0), self.buf(3), **{self.axis: 1})
            self.left = send(self.buf(0), self.buf(1), **{self.axis: 3})

        def mid(self):
            self.right.wait_recv()
            self.far_right = send(self.first(self.buf(3)), self.first(self.buf(2)), **{self.axis: 1})
            self.left.wait_recv()
            self.far_left = send(self.second(self.buf(1)), self.second(self.buf(2)), **{self.axis: 3})

        def finish(self):
            self.far_right.wait_recv()
            self.far_left.wait_recv()

    class Scatter:
        def __init__(self, axis, part, relay, full, first, second):
            self.axis, self.part, self.relay, self.full = axis, part, relay, full
            self.first, self.second = first, second

        def start(self):
            self.a = send(self.first(self.part(2)), self.relay(0), **{self.axis: 1})
            self.b = send(self.second(self.part(2)), self.relay(1), **{self.axis: 3})

        def mid(self):
            self.a.wait_recv()
            piece = self.first(self.part(1))
            piece[...] = (piece[...].astype(F32) + self.relay(0)[...].astype(F32)).astype(BF)
            self.right = send(self.part(1), self.full(0), **{self.axis: 1})
            self.b.wait_recv()
            piece = self.second(self.part(3))
            piece[...] = (piece[...].astype(F32) + self.relay(1)[...].astype(F32)).astype(BF)
            self.left = send(self.part(3), self.full(1), **{self.axis: 3})

        def finish(self):
            self.right.wait_recv()
            self.left.wait_recv()
            return (
                self.part(0)[...].astype(F32)
                + self.full(0)[...].astype(F32)
                + self.full(1)[...].astype(F32)
            )

    class Reduce:
        def __init__(self, parts, core, sums, lands, out):
            self.parts, self.core, self.sums, self.lands, self.out = parts, core, sums, lands, out

        def start(self):
            self.pair = send(self.parts.at[1 - c], self.core, dc=1)

        def mid(self):
            self.pair.wait_recv()
            self.sums[...] = (
                self.parts[c].astype(F32) + self.core[...].astype(F32)
            ).astype(BF)
            self.hops = [
                send(self.sums.at[(l + i) % 4], self.lands.at[i - 1], dl=i) for i in (1, 2, 3)
            ]

        def finish(self):
            total = self.sums[l].astype(F32)
            for i, hop in enumerate(self.hops):
                hop.wait_recv()
                total = total + self.lands[i].astype(F32)
            return total.astype(BF)

        def share(self):
            self.out[c, l] = self.finish()
            self.back = [
                send(self.out.at[c, l], self.out.at[c, l], dl=i) for i in (1, 2, 3)
            ]

        def across(self):
            for hop in self.back:
                hop.wait_recv()
            self.other = send(self.out.at[c], self.out.at[c], dc=1)

        def done(self):
            self.other.wait_recv()

    def rows(lo, hi):
        return lambda ref: ref.at[lo:hi]

    s["xb"][0, 0, 0:FEAT] = tokens[...].T
    routes_t = routes[...].astype(F32).T
    s["xb"][0, 0, FEAT:XROWS] = jnp.concatenate(
        [routes_t, jnp.zeros((8, TOK), F32)], axis=0
    ).astype(BF)
    x_halves = rows(0, 256), rows(256, XROWS)
    xh = Gather("dh", lambda i: s["xb"].at[i, 0], *x_halves)
    xy = [Gather("dy", lambda i, q=q: s["xb"].at[q, i], *x_halves) for q in range(4)]
    xh.start()
    xy[0].start()
    s["wb"][0, 0:512] = gleft[0]
    s["wb"][0, 512:1024] = uleft[0]
    s["wb"][0, 1024:1120] = gright[0].astype(F32).T.astype(BF)
    s["wb"][0, 1120:1216] = uright[0].astype(F32).T.astype(BF)
    w_halves = rows(0, WROWS // 2), rows(WROWS // 2, WROWS)
    wx = Gather("dx", lambda i: s["wb"].at[i], *w_halves)
    wx.start()

    for half, base in enumerate((gbase, ubase)):
        part = dot(tokens[...], base[...]).T.astype(BF)
        for place in range(4):
            for core in range(2):
                lo = (place * 2 + core) * HID
                s["ap"][place, core, half * HID : (half + 1) * HID] = part[lo : lo + HID]

    class ActReduce(Reduce):
        def start(self):
            self.pair = send(s["ap"].at[:, 1 - c], self.core, dc=1)

        def mid(self):
            self.pair.wait_recv()
            self.sums[...] = (s["ap"][:, c].astype(F32) + self.core[...].astype(F32)).astype(BF)
            self.hops = [
                send(self.sums.at[(l + i) % 4], self.lands.at[i - 1], dl=i) for i in (1, 2, 3)
            ]

    act = ActReduce(None, s["ac"], s["as_"], s["az"], None)
    act.start()
    xy[0].mid()
    wx.mid()

    upper = (iota((TOK, TOK), 0) < iota((TOK, TOK), 1)).astype(BF)
    ranks = iota((64, TOK), 0)
    names = (
        ((x + ranks % 4) % 4) * 16 + ((y + (ranks // 4) % 4) % 4) * 4 + (h + ranks // 16) % 4
    ).astype(F32)
    chosen = [(names == routes_t[k : k + 1]).astype(F32) for k in range(8)]
    ranks_f = ranks.astype(F32)
    order = dot(sum(chosen).astype(BF), upper) + ranks_f * CAP
    slot = [jnp.sum(chosen[k] * order, axis=0, keepdims=True) for k in range(8)]
    hid = hidden[...].reshape(8 * TOK, HID)
    hid_t = jnp.transpose(hidden[...].astype(F32), (1, 2, 0)).astype(BF)
    hid_t = jnp.concatenate([hid_t[k] for k in range(8)], axis=1)
    for place in range(16):
        want = (iota((TOK, TOK), 0) + place * TOK).astype(F32)
        pick = jnp.concatenate([(slot[k] == want).astype(BF) for k in range(8)], axis=1)
        s["ho"][place // 4, place % 4] = dot(hid_t, pick, 1, 1).astype(BF)
    s["hb"][0, 0] = s["ho"][0, 0]
    hh = [None] + [send(s["ho"].at[i], s["hm"].at[4 - i], dh=i) for i in (1, 2, 3)]
    hy = {0: [send(s["ho"].at[0, i], s["hb"].at[0, 4 - i], dy=i) for i in (1, 2, 3)]}

    def pass_hidden(i):
        hh[4 - i].wait_recv()
        s["hb"][i, 0] = s["hm"][i, 0]
        hy[i] = [send(s["hm"].at[i, j], s["hb"].at[i, 4 - j], dy=j) for j in (1, 2, 3)]

    act.mid()
    r4, c4 = iota((512, 512), 0), iota((512, 512), 1)
    s["pm"][...] = (
        (r4 // 128 == (c4 // 32) % 4) & ((r4 // 32) % 4 == c4 // 128) & (r4 % 32 == c4 % 32)
    ).astype(BF)
    s["pb"][...] = jnp.zeros_like(s["pb"])

    xh.mid()
    xy[1].start()
    xy[3].start()

    s["ab"][0, 0] = act.finish()
    a_halves = rows(0, HID), rows(HID, 2 * HID)
    ah = Gather("dh", lambda i: s["ab"].at[i, 0], *a_halves)
    ay = [Gather("dy", lambda i, q=q: s["ab"].at[q, i], *a_halves) for q in range(4)]
    ah.start()
    ay[0].start()

    experts = [(((x + j) % 4) * 16 + y * 4 + h).astype(F32) for j in range(4)]
    group_sum = (iota((16, TOK), 1) // 8 == iota((16, TOK), 0)).astype(BF)

    def select(q):
        named = []
        for b in range(4):
            block = s["xb"][q, b, FEAT:XROWS].astype(F32)[0:8]
            named += [(block == experts[j]).astype(F32) for j in range(4)]
        hit = dot(group_sum, jnp.concatenate(named, axis=0).astype(BF))
        place = jnp.where(hit > 0.5, dot(hit.astype(BF), upper), -1.0)
        want = iota((CAP, TOK), 0).astype(F32)
        for b in range(4):
            for j in range(4):
                row = place[b * 4 + j : b * 4 + j + 1]
                s["pb"][q, j * 128 + b * CAP : j * 128 + (b + 1) * CAP, b * TOK : (b + 1) * TOK] = (
                    row == want
                ).astype(BF)
        feats = jnp.concatenate([s["xb"][q, b, 0:FEAT] for b in range(4)], axis=1)
        s["xs"][q] = dot(feats, s["pb"][q], 1, 1).astype(BF)
        for j in range(4):
            low = dot(s["lt"][j], s["xs"][q, :, j * TOK : (j + 1) * TOK]).astype(BF)
            s["lp"][q, 0, j] = low[0:R]
            s["lp"][q, 1, j] = low[R : 2 * R]

    low = [
        Reduce(s["lp"].at[q], s["lc"].at[q], s["ls"].at[q], s["lz"].at[q], s["lo"].at[q])
        for q in range(4)
    ]
    dlow = [
        Reduce(s["kp"].at[q], s["kc"].at[q], s["ks"].at[q], s["kz"].at[q], s["ko"].at[q])
        for q in range(4)
    ]

    wx.finish()
    for j in range(4):
        s["lt"][j, 0:R] = s["wb"][j, 0:512].T
        s["lt"][j, R : 2 * R] = s["wb"][j, 512:1024].T
    xy[0].finish()
    select(0)
    low[0].start()
    xy[1].mid()
    xy[3].mid()
    xh.finish()
    xy[2].start()
    low[0].mid()
    ah.mid()
    ay[1].start()
    ay[3].start()
    ay[0].mid()
    xy[1].finish()
    select(1)
    low[1].start()
    xy[2].mid()
    low[0].share()
    low[1].mid()
    xy[3].finish()
    select(3)
    low[3].start()
    ay[1].mid()
    ay[3].mid()
    ah.finish()
    ay[2].start()
    low[1].share()
    low[0].across()
    low[3].mid()
    xy[2].finish()
    select(2)
    low[2].start()
    ay[2].mid()
    low[3].share()
    low[1].across()
    low[2].mid()
    for i in (1, 3, 2):
        pass_hidden(i)
    low[2].share()
    low[3].across()
    low[2].across()

    def middle(q):
        for j in (1, 2, 3):
            hy[q][j - 1].wait_recv()
        acts = jnp.concatenate([s["ab"][q, b] for b in range(4)], axis=1)
        acts = dot(acts, s["pb"][q], 1, 1)
        cot = jnp.concatenate([s["hb"][q, b] for b in range(4)], axis=1)
        cot = dot(cot, s["pm"][...], 1, 1)
        gate = acts[0:HID] + jnp.concatenate(
            [dot(s["wb"][j, 1024:1120], s["lo"][q, 0, j]) for j in range(4)], axis=1
        )
        up = acts[HID : 2 * HID] + jnp.concatenate(
            [dot(s["wb"][j, 1120:1216], s["lo"][q, 1, j]) for j in range(4)], axis=1
        )
        sigma = jax.nn.sigmoid(gate)
        s["dg"][q, 0:HID] = (cot * up * sigma * (1.0 + gate * (1.0 - sigma))).astype(BF)
        s["dg"][q, HID : 2 * HID] = (cot * gate * sigma).astype(BF)
        for j in range(4):
            for half in range(2):
                s["kp"][q, half, j] = dot(
                    s["wb"][j, 1024 + half * HID : 1120 + half * HID],
                    s["dg"][q, half * HID : (half + 1) * HID, j * TOK : (j + 1) * TOK],
                    0,
                    0,
                ).astype(BF)

    def sums(q):
        part = dot(s["dg"][q], s["pb"][q]).astype(BF)
        for b in range(4):
            s["gp"][q, b] = part[:, b * TOK : (b + 1) * TOK]

    gy = [
        Scatter(
            "dy",
            lambda i, q=q: s["gp"].at[q, i],
            lambda i, q=q: s["gr"].at[q, i],
            lambda i, q=q: s["gf"].at[q, i],
            *a_halves,
        )
        for q in range(4)
    ]
    gh = Scatter(
        "dh", lambda i: s["gq"].at[i], lambda i: s["hr"].at[i], lambda i: s["hf"].at[i], *a_halves
    )
    d_halves = rows(0, 256), rows(256, 512)
    dy = [
        Scatter(
            "dy",
            lambda i, q=q: s["dp"].at[q, i],
            lambda i, q=q: s["dr"].at[q, i],
            lambda i, q=q: s["df"].at[q, i],
            *d_halves,
        )
        for q in range(4)
    ]
    dh = Scatter(
        "dh", lambda i: s["dq"].at[i], lambda i: s["er"].at[i], lambda i: s["ef"].at[i], *d_halves
    )

    def inputs(q):
        part = None
        for j in range(4):
            left = jnp.concatenate([s["wb"][j, 0:512], s["wb"][j, 512:1024]], axis=1)
            back = jnp.concatenate([s["ko"][q, 0, j], s["ko"][q, 1, j]], axis=0)
            s["dp"][q, j] = dot(left, back).astype(BF)
        delta = jnp.concatenate([s["dp"][q, j] for j in range(4)], axis=1)
        part = dot(delta, s["pb"][q]).astype(BF)
        for b in range(4):
            s["dp"][q, b] = part[:, b * TOK : (b + 1) * TOK]

    xy_left = [ay[0], ay[1], ay[3], ay[2]]
    back_order = (2, 1, 3, 0)
    low_done = set()
    for q in (0, 1, 3, 2):
        low[q].done()
    for a in xy_left:
        a.finish()
    for n, q in enumerate(back_order):
        middle(q)
        dlow[q].start()
        sums(q)
        gy[q].start()
        if n >= 1:
            p = back_order[n - 1]
            dlow[p].mid()
            gy[p].mid()
        if n >= 2:
            p = back_order[n - 2]
            dlow[p].share()
            s["gq"][p] = gy[p].finish().astype(BF)
            if p == 2:
                gh.start()
    dlow[0].mid()
    gy[0].mid()
    dlow[2].across()
    dlow[3].share()
    s["gq"][3] = gy[3].finish().astype(BF)
    gh.mid()
    dlow[1].across()
    dlow[0].share()
    s["gq"][0] = gy[0].finish().astype(BF)
    dlow[2].done()
    inputs(2)
    dy[2].start()
    dlow[3].across()
    dlow[1].done()
    inputs(1)
    dy[1].start()
    dy[2].mid()
    dlow[0].across()
    total = gh.finish().astype(BF)
    s["gs"][0, l, c] = total[0:HID]
    s["gs"][1, l, c] = total[HID : 2 * HID]
    gs_back = [
        send(s["gs"].at[:, l, c], s["gs"].at[:, l, c], dl=i) for i in (1, 2, 3)
    ]
    dlow[3].done()
    inputs(3)
    dy[3].start()
    dy[1].mid()
    s["dq"][2] = dy[2].finish().astype(BF)
    dh.start()
    for hop in gs_back:
        hop.wait_recv()
    gs_core = send(s["gs"].at[:, :, c], s["gs"].at[:, :, c], dc=1)
    dlow[0].done()
    inputs(0)
    dy[0].start()
    dy[3].mid()
    s["dq"][1] = dy[1].finish().astype(BF)
    s["dq"][3] = dy[3].finish().astype(BF)
    dh.mid()
    dy[0].mid()

    gs_core.wait_recv()
    whole = [s["gs"][half].reshape(FF, TOK) for half in range(2)]
    feats_t = s["xb"][0, 0, 0:FEAT]
    for place in range(4):
        piece = feats_t[place * 128 : (place + 1) * 128]
        both = jnp.concatenate(
            [dot(piece, whole[half], 1, 1).reshape(16, 8, FF) for half in range(2)], axis=1
        )
        s["bg"][place] = both.astype(BF).reshape(4, 4, 16, FF)

    bx = Scatter(
        "dx",
        lambda i: s["bg"].at[(x + i) % 4],
        lambda i: s["bxr"].at[i],
        lambda i: s["bxf"].at[i],
        rows(0, 2),
        rows(2, 4),
    )
    bx.start()

    for j in range(4):
        slots = jnp.concatenate(
            [s["xs"][q, :, j * TOK : (j + 1) * TOK] for q in range(4)], axis=1
        )
        for half in range(2):
            back = jnp.concatenate([s["ko"][q, half, j] for q in range(4)], axis=1)
            s["wg"][j, half * 512 : (half + 1) * 512] = dot(slots, back, 1, 1).astype(BF)
            lows = jnp.concatenate([s["lo"][q, half, j] for q in range(4)], axis=1)
            dgs = jnp.concatenate(
                [
                    s["dg"][q, half * HID : (half + 1) * HID, j * TOK : (j + 1) * TOK]
                    for q in range(4)
                ],
                axis=1,
            )
            s["wg"][j, 1024 + half * HID : 1120 + half * HID] = dot(dgs, lows, 1, 1).astype(BF)
    wgx = Scatter(
        "dx", lambda i: s["wg"].at[i], lambda i: s["wr"].at[i], lambda i: s["wf"].at[i], *w_halves
    )
    wgx.start()
    bx.mid()
    s["dq"][0] = dy[0].finish().astype(BF)
    wgx.mid()
    base_part = dot(gbase[...], whole[0]) + dot(ubase[...], whole[1])
    s["by"][...] = bx.finish().astype(BF)
    by = Scatter(
        "dy",
        lambda i: s["by"].at[(y + i) % 4],
        lambda i: s["byr"].at[i],
        lambda i: s["byf"].at[i],
        rows(0, 2),
        rows(2, 4),
    )
    by.start()
    o_tok[...] = (dh.finish() + base_part).T.astype(BF)
    by.mid()
    s["bz"][...] = by.finish().astype(BF)
    bz = Scatter(
        "dh",
        lambda i: s["bz"].at[(h + i) % 4],
        lambda i: s["bzr"].at[i],
        lambda i: s["bzf"].at[i],
        lambda ref: ref.at[:, 0 : FF // 2],
        lambda ref: ref.at[:, FF // 2 : FF],
    )
    bz.start()
    grads = wgx.finish()
    o_gl[0] = grads[0:512]
    o_ul[0] = grads[512:1024]
    o_gr[0] = grads[1024:1120].T
    o_ur[0] = grads[1120:1216].T
    bz.mid()
    grad = bz.finish()
    o_gb[...] = grad[0:8]
    o_ub[...] = grad[8:16]
    for copy in started:
        copy.wait_send()


def local(*args):
    vmem = pl.BlockSpec(memory_space=pltpu.VMEM)
    shapes = [
        ((TOK, FEAT), BF),
        ((8, FF), F32),
        ((8, FF), F32),
        ((1, FEAT, R), F32),
        ((1, FEAT, R), F32),
        ((1, R, HID), F32),
        ((1, R, HID), F32),
    ]
    return pl.pallas_call(
        kernel,
        out_shape=[jax.ShapeDtypeStruct(*shape) for shape in shapes],
        in_specs=[vmem] * 9,
        out_specs=[vmem] * 7,
        scratch_shapes=[pltpu.VMEM(*shape) for shape in SCRATCH.values()]
        + [pltpu.SemaphoreType.DMA((SEMS,)), pltpu.SemaphoreType.DMA((SEMS,))],
        compiler_params=pltpu.CompilerParams(
            collective_id=0, has_side_effects=True, vmem_limit_bytes=56 * 1024 * 1024
        ),
    )(*args)


def solution(mesh):
    return jax.shard_map(
        local,
        mesh=mesh,
        in_specs=(
            P("expert", "fsdp"),
            P("expert", None),
            P("expert", None, "fsdp"),
            P("fsdp", None),
            P("fsdp", None),
            P("expert", "fsdp", None),
            P("expert", "fsdp", None),
            P("expert", None, "fsdp"),
            P("expert", None, "fsdp"),
        ),
        out_specs=(
            P("expert", "fsdp"),
            P(("fsdp", "expert"), None),
            P(("fsdp", "expert"), None),
            P("expert", "fsdp", None),
            P("expert", "fsdp", None),
            P("expert", None, "fsdp"),
            P("expert", None, "fsdp"),
        ),
        check_vma=False,
    )
```

```python
import types

import jax
import jax.numpy as jnp
from jax import lax
from jax.experimental import pallas as pl
from jax.experimental.pallas import tpu as pltpu
from jax.sharding import PartitionSpec as P

BF = jnp.bfloat16
F32 = jnp.float32
MESH = pl.DeviceIdType.MESH
TOK = 128
FEAT = 512
HID = 96
FF = 768
R = 128
CAP = 32
XROWS = 528
WROWS = 1216
SEMS = 288


def dot(a, b, ca=1, cb=0):
    return lax.dot_general(a, b, (((ca,), (cb,)), ((), ())), preferred_element_type=F32)


def iota(shape, dim):
    return lax.broadcasted_iota(jnp.int32, shape, dim)


SCRATCH = dict(
    hi=((8, HID, TOK), BF),
    gi=((FEAT, FF), BF),
    ui=((FEAT, FF), BF),
    xb=((4, 4, XROWS, TOK), BF),
    wb=((4, WROWS, R), BF),
    lt=((4, 2 * R, FEAT), BF),
    ap=((2, 4, 2 * HID, TOK), F32),
    ac=((4, 2 * HID, TOK), F32),
    as_=((4, 2 * HID, TOK), BF),
    az=((3, 2 * HID, TOK), BF),
    ab=((4, 4, 2 * HID, TOK), BF),
    ho=((4, 4, HID, TOK), BF),
    hw=((2, 2, HID, TOK), BF),
    hm=((4, 4, HID, TOK), BF),
    hb=((4, 4, HID, TOK), BF),
    pm=((4 * TOK, 4 * TOK), BF),
    pb=((4, 4 * TOK, 4 * TOK), BF),
    xs=((4, FEAT, 4 * TOK), BF),
    lp=((4, 2, 4, R, TOK), F32),
    lc=((4, 4, R, TOK), F32),
    ls=((4, 4, R, TOK), BF),
    lz=((4, 2, 4, R, TOK), BF),
    lo=((4, 2, 4, R, TOK), BF),
    kp=((4, 2, 4, R, TOK), F32),
    kc=((4, 4, R, TOK), F32),
    ks=((4, 4, R, TOK), BF),
    kz=((4, 2, 4, R, TOK), BF),
    ko=((4, 2, 4, R, TOK), BF),
    dg=((4, 2 * HID, 4 * TOK), BF),
    gp=((4, 4, 2 * HID, TOK), BF),
    gw=((4, 4, 2 * HID, TOK), F32),
    gf=((4, 3, 2 * HID, TOK), BF),
    gq=((4, 2 * HID, TOK), BF),
    gv=((4, 2 * HID, TOK), F32),
    hr=((2, HID, TOK), BF),
    hf=((2, 2 * HID, TOK), BF),
    gs=((2, 4, 2, HID, TOK), BF),
    dp=((2, 4, 4, FEAT // 2, TOK), BF),
    dw=((2, 4, 4, FEAT // 2, TOK), F32),
    dr=((2, 4, 2, FEAT // 4, TOK), BF),
    df=((2, 4, 2, FEAT // 2, TOK), BF),
    dq=((2, 4, FEAT // 2, TOK), BF),
    dv=((2, 4, FEAT // 2, TOK), F32),
    er=((2, 2, FEAT // 4, TOK), BF),
    ef=((2, 2, FEAT // 2, TOK), BF),
    wg=((4, WROWS, R), BF),
    ww=((4, WROWS, R), F32),
    wr=((2, WROWS // 2, R), BF),
    wf=((2, WROWS, R), BF),
    bg=((2, 4, 4, 4, 16, FF // 2), BF),
    bw=((2, 4, 4, 4, 16, FF // 2), F32),
    bxr=((2, 2, 2, 4, 16, FF // 2), BF),
    bxf=((2, 2, 4, 4, 16, FF // 2), BF),
    by=((2, 4, 4, 16, FF // 2), BF),
    byw=((2, 4, 4, 16, FF // 2), F32),
    byf=((2, 3, 4, 16, FF // 2), BF),
    bz=((2, 4, 16, FF // 2), BF),
    bzw=((2, 4, 16, FF // 2), F32),
    bzf=((2, 3, 16, FF // 2), BF),
)


ORDER = (
    0, 3, 15, 20, 21, 22, 16, 17, 1, 9, 4, 18, 19, 40, 23, 24, 27, 6, 5, 48, 49, 50, 51, 2, 12, 39, 41, 10, 28, 11,
    7, 52, 44, 100, 101, 102, 13, 103, 25, 33, 14, 126, 8, 74, 34, 127, 30, 128, 129, 47, 53, 104, 35, 42, 75, 76,
    54, 77, 45, 130, 105, 43, 29, 55, 56, 57, 31, 26, 36, 63, 131, 58, 78, 64, 106, 107, 37, 108, 109, 115, 46, 110,
    38, 116, 132, 79, 59, 133, 134, 135, 141, 142, 136, 111, 80, 32, 60, 81, 82, 83, 89, 90, 137, 84, 112, 143, 152,
    61, 62, 70, 71, 138, 85, 91, 117, 153, 113, 65, 114, 66, 67, 122, 118, 119, 123, 86, 139, 140, 144, 148, 145,
    149, 120, 154, 155, 124, 150, 87, 88, 173, 92, 93, 96, 97, 174, 156, 151, 183, 146, 98, 157, 158, 68, 165, 166,
    147, 178, 99, 125, 184, 159, 94, 95, 121, 167, 175, 179, 160, 161, 162, 163, 168, 169, 170, 171, 72, 164, 73,
    182, 185, 186, 176, 69, 180, 177, 181, 172,
)


class Plan:
    def __init__(self):
        self.steps = {}

    def add(self, name, run, after=(), cost=0.1, link=None, size=0.0):
        assert name not in self.steps
        self.steps[name] = (run, tuple(after), cost, link, size)

    def order(self):
        names, done = list(self.steps), set()
        assert sorted(ORDER) == list(range(len(names)))
        for place in ORDER:
            assert all(dep.lstrip(">") in done for dep in self.steps[names[place]][1])
            done.add(names[place])
        return [names[place] for place in ORDER]


def kernel(*refs):
    (tokens, routes, hidden_in, gbase_in, ubase_in, gleft, uleft, gright, uright) = refs[:9]
    (o_tok, o_gb, o_ub, o_gl, o_ul, o_gr, o_ur) = refs[9:16]
    s = types.SimpleNamespace(**dict(zip(SCRATCH, refs[16 : 16 + len(SCRATCH)])))
    send_sem, recv_sem, read_sem = refs[16 + len(SCRATCH) :]
    hidden, gbase, ubase = s.hi, s.gi, s.ui

    e = lax.axis_index("expert")
    f = lax.axis_index("fsdp")
    x, y, h = e // 16, (e // 4) % 4, e % 4
    l, c = f // 2, f % 2

    def at(dx=0, dy=0, dh=0, dl=0, dc=0):
        return (
            ((x + dx) % 4) * 16 + ((y + dy) % 4) * 4 + (h + dh) % 4,
            ((l + dl) % 4) * 2 + (c + dc) % 2,
        )

    peers = [dict(dx=1), dict(dx=3), dict(dy=1), dict(dy=2), dict(dy=3), dict(dh=1), dict(dh=2), dict(dh=3)]
    peers += [dict(dl=1), dict(dl=2), dict(dl=3), dict(dc=1)]
    barrier = pltpu.get_barrier_semaphore()
    for peer in peers:
        pl.semaphore_signal(barrier, inc=1, device_id=at(**peer), device_id_type=MESH)

    reads = [
        pltpu.make_async_copy(src, dst, read_sem.at[n])
        for n, (src, dst) in enumerate(
            [
                (gleft.at[0], s.wb.at[0, 0:512]),
                (uleft.at[0], s.wb.at[0, 512:1024]),
                (gright.at[0], s.wb.at[0, 1024:1120]),
                (uright.at[0], s.wb.at[0, 1120:1216]),
                (gbase_in, gbase),
                (ubase_in, ubase),
                (hidden_in, hidden),
            ]
        )
    ]
    for read in reads:
        read.start()

    started = []

    class Copy:
        def __init__(self, src, dst, here, there, where):
            self.src, self.dst, self.here, self.there, self.where = src, dst, here, there, where
            self.n = len(started)
            started.append(self)
            self.run(here, lambda copy: copy.start())

        def run(self, when, act):
            def go():
                act(
                    pltpu.make_async_remote_copy(
                        src_ref=self.src,
                        dst_ref=self.dst,
                        send_sem=send_sem.at[self.n],
                        recv_sem=recv_sem.at[self.n],
                        device_id=at(**self.where),
                        device_id_type=MESH,
                    )
                )

            if when is None:
                go()
            else:
                pl.when(when)(go)

        def wait_recv(self):
            self.run(self.there, lambda copy: copy.wait_recv())

        def wait_send(self):
            self.run(self.here, lambda copy: copy.wait_send())

    def send(src, dst, here=None, there=None, **where):
        return Copy(src, dst, here, there, where)

    edge, inner = (l == 0) | (l == 3), (l == 1) | (l == 2)

    class Gather:
        def __init__(self, axis, buf, first, second):
            self.axis, self.buf, self.first, self.second = axis, buf, first, second

        def start(self):
            self.right = send(self.buf(0), self.buf(3), **{self.axis: 1})
            self.left = send(self.buf(0), self.buf(1), **{self.axis: 3})

        def mid(self):
            self.right.wait_recv()
            self.far_right = send(self.first(self.buf(3)), self.first(self.buf(2)), **{self.axis: 1})
            self.left.wait_recv()
            self.far_left = send(self.second(self.buf(1)), self.second(self.buf(2)), **{self.axis: 3})

        def finish(self):
            self.far_right.wait_recv()
            self.far_left.wait_recv()

    class Scatter:
        def __init__(self, axis, part, wide, relay, full, first, second):
            self.axis, self.part, self.wide, self.relay, self.full = axis, part, wide, relay, full
            self.first, self.second = first, second

        def start(self):
            self.a = send(self.first(self.part(2)), self.relay(0), **{self.axis: 1})
            self.b = send(self.second(self.part(2)), self.relay(1), **{self.axis: 3})

        def mid(self):
            for copy, half, i in ((self.a, self.first, 1), (self.b, self.second, 3)):
                copy.wait_recv()
                lane = self.relay(i // 2)[...].astype(F32)
                half(self.part(i))[...] = (half(self.wide(i))[...] + lane).astype(BF)
            self.right = send(self.part(1), self.full(0), **{self.axis: 1})
            self.left = send(self.part(3), self.full(1), **{self.axis: 3})

        def finish(self):
            self.right.wait_recv()
            self.left.wait_recv()
            return (
                self.wide(0)[...]
                + self.full(0)[...].astype(F32)
                + self.full(1)[...].astype(F32)
            )

    class Direct:
        def __init__(self, axis, part, wide, full):
            self.axis, self.part, self.wide, self.full = axis, part, wide, full

        def start(self):
            self.copies = [
                send(self.part(i), self.full(i - 1), **{self.axis: i}) for i in (1, 3, 2)
            ]

        def finish(self):
            total = self.wide(0)[...]
            for i, copy in zip((1, 3, 2), self.copies):
                copy.wait_recv()
                total = total + self.full(i - 1)[...].astype(F32)
            return total

    class Reduce:
        def __init__(self, parts, core, sums, lands):
            self.parts, self.core, self.sums, self.lands = parts, core, sums, lands

        def start(self):
            self.pair = send(self.parts.at[1 - c], self.core, dc=1)

        def mid(self):
            self.pair.wait_recv()
            total = self.parts[c] + self.core[...]
            self.parts[c] = total
            self.sums[...] = total.astype(BF)
            self.hops = [
                send(self.sums.at[(l + i) % 4], self.lands.at[i - 1], dl=i) for i in (1, 2, 3)
            ]

        def finish(self):
            total = self.parts[c, l]
            for i, hop in enumerate(self.hops):
                hop.wait_recv()
                total = total + self.lands[i].astype(F32)
            return total.astype(BF)

    class AllReduce:
        def __init__(self, parts, core, sums, lands, out):
            self.parts, self.core, self.sums, self.lands, self.out = parts, core, sums, lands, out

        def start(self):
            self.pair = send(self.parts.at[1 - c], self.core, dc=1)

        def outer(self):
            self.pair.wait_recv()
            total = self.parts[c] + self.core[...]
            self.parts[c] = total

            @pl.when(edge)
            def _():
                self.sums[...] = total.astype(BF)

            self.up = send(self.sums, self.lands.at[0], edge, inner, dl=1 - 2 * (l % 2))

        def swap(self):
            self.up.wait_recv()

            @pl.when(inner)
            def _():
                total = self.parts[c] + self.lands[0].astype(F32)
                self.parts[c] = total
                self.sums[...] = total.astype(BF)

            self.over = send(self.sums, self.lands.at[1], inner, inner, dl=3 - 2 * l)

        def share(self):
            self.over.wait_recv()

            @pl.when(inner)
            def _():
                self.out[c] = (self.parts[c] + self.lands[1].astype(F32)).astype(BF)

            self.down = send(self.out.at[c], self.out.at[c], inner, edge, dl=1 - 2 * (l % 2))
            self.inner_pair = send(self.out.at[c], self.out.at[c], inner, inner, dc=1)

        def across(self):
            self.down.wait_recv()
            self.edge_pair = send(self.out.at[c], self.out.at[c], edge, edge, dc=1)

        def done(self):
            self.inner_pair.wait_recv()
            self.edge_pair.wait_recv()

    def rows(lo, hi):
        return lambda ref: ref.at[lo:hi]

    routes_t = routes[...].astype(F32)
    s.xb[0, 0, 0:FEAT] = tokens[...].T
    s.xb[0, 0, FEAT:XROWS] = jnp.concatenate(
        [routes_t, jnp.zeros((8, TOK), F32)], axis=0
    ).astype(BF)
    pl.semaphore_wait(barrier, len(peers))

    plan = Plan()

    upper = (iota((TOK, TOK), 0) < iota((TOK, TOK), 1)).astype(BF)

    def own_weights():
        for read in reads[0:4]:
            read.wait()

    def own_partials():
        reads[4].wait()
        reads[5].wait()
        for half, base in enumerate((gbase, ubase)):
            part = dot(tokens[...], base[...]).T
            for place in range(4):
                for core in range(2):
                    lo = (place * 2 + core) * HID
                    s.ap[core, place, half * HID : (half + 1) * HID] = part[lo : lo + HID]

    def own_slots():
        reads[6].wait()
        ranks = iota((64, TOK), 0)
        names = (
            ((x + ranks % 4) % 4) * 16 + ((y + (ranks // 4) % 4) % 4) * 4 + (h + ranks // 16) % 4
        ).astype(F32)
        chosen = [(names == routes_t[k : k + 1]).astype(F32) for k in range(8)]
        order = dot(sum(chosen).astype(BF), upper) + ranks.astype(F32) * CAP
        slot = [jnp.sum(chosen[k] * order, axis=0, keepdims=True) for k in range(8)]
        hid_t = jnp.concatenate([hidden[k] for k in range(8)], axis=1)
        for place in range(16):
            want = (iota((TOK, TOK), 0) + place * TOK).astype(F32)
            pick = jnp.concatenate([(slot[k] == want).astype(BF) for k in range(8)], axis=1)
            s.ho[place // 4, place % 4] = dot(hid_t, pick, 1, 1).astype(BF)
        s.hb[0, 0] = s.ho[0, 0]

    def tables():
        r4, c4 = iota((512, 512), 0), iota((512, 512), 1)
        s.pm[...] = (
            (r4 // 128 == (c4 // 32) % 4) & ((r4 // 32) % 4 == c4 // 128) & (r4 % 32 == c4 % 32)
        ).astype(BF)
        s.pb[...] = jnp.zeros_like(s.pb)

    def gather(name, task, link, size, after=()):
        plan.add(name + "0", task.start, after, 0.1, link, size)
        plan.add(name + "1", task.mid, [">" + name + "0"], 0.1, link, size / 2)
        plan.add(name + "2", task.finish, [">" + name + "1"], 0.05)

    def scatter(name, task, link, size, after, last, cost=0.3):
        plan.add(name + "0", task.start, after, 0.1, link, size / 2)
        plan.add(name + "1", task.mid, [">" + name + "0"] + list(after), cost, link, size)
        plan.add(name + "2", last, [">" + name + "1"], cost)

    def direct(name, task, link, size, after, last, cost=0.2):
        plan.add(name + "0", task.start, after, 0.1, link, size)
        plan.add(name + "2", last, [">" + name + "0"], cost)

    x_halves = rows(0, 256), rows(256, XROWS)
    gather("xh", Gather("dh", lambda i: s.xb.at[i, 0], *x_halves), "z", 1.0)
    for q in (0, 1, 3, 2):
        task = Gather("dy", lambda i, q=q: s.xb.at[q, i], *x_halves)
        gather(f"xy{q}", task, "y", 0.25, [[], ["xh1"], ["xh2"], ["xh1"]][q])
    plan.add("wts", own_weights, [], 0.2)
    w_halves = rows(0, WROWS // 2), rows(WROWS // 2, WROWS)
    gather("wx", Gather("dx", lambda i: s.wb.at[i], *w_halves), "x", 0.6, ["wts"])

    def turn():
        for j in range(4):
            s.lt[j, 0:R] = s.wb[j, 0:512].T
            s.lt[j, R : 2 * R] = s.wb[j, 512:1024].T

    plan.add("lt", turn, ["wx2"], 0.5)

    act = Reduce(s.ap, s.ac, s.as_, s.az)

    def own_act():
        s.ab[0, 0] = act.finish()

    plan.add("actp", own_partials, [], 0.8)
    plan.add("act0", act.start, ["actp"], 0.1, "core", 0.375)
    plan.add("act1", act.mid, [">act0"], 0.3, "z", 0.375)
    plan.add("act2", own_act, [">act1"], 0.2)
    a_halves = rows(0, HID), rows(HID, 2 * HID)
    gather("ah", Gather("dh", lambda i: s.ab.at[i, 0], *a_halves), "z", 0.375, ["act2"])
    for q in (0, 1, 3, 2):
        task = Gather("dy", lambda i, q=q: s.ab.at[q, i], *a_halves)
        gather(f"ay{q}", task, "y", 0.1, [["act2"], ["ah1"], ["ah2"], ["ah1"]][q])

    hop = {}

    def hidden_near():
        hop["near"] = [send(s.ho.at[i], s.hm.at[4 - i], dh=i) for i in (1, 3)]

    def hidden_far():
        hop["far"] = [
            send(s.ho.at[2, 0:2], s.hw.at[0], dh=1),
            send(s.ho.at[2, 2:4], s.hw.at[1], dh=3),
        ]

    def hidden_on():
        hop["on"] = []
        for n, copy in enumerate(hop["far"]):
            copy.wait_recv()
            hop["on"].append(
                send(s.hw.at[n], s.hm.at[2, 2 * n : 2 * n + 2], dh=(1, 3)[n])
            )

    def hidden_pass(q):
        if q in (1, 3):
            hop["near"][{3: 0, 1: 1}[q]].wait_recv()
        elif q == 2:
            for copy in hop["on"]:
                copy.wait_recv()
        held = s.ho if q == 0 else s.hm
        if q:
            s.hb[q, 0] = s.hm[q, 0]
        hop[q] = [send(held.at[q, j], s.hb.at[q, 4 - j], dy=j) for j in (1, 2, 3)]

    plan.add("slots", own_slots, [], 1.5)
    plan.add("tab", tables, [], 0.4)
    plan.add("hn", hidden_near, ["slots", "xh1"], 0.1, "z", 0.75)
    plan.add("hf", hidden_far, ["slots", "xh1"], 0.1, "z", 0.375)
    plan.add("ho", hidden_on, [">hf"], 0.1, "z", 0.375)
    for q in range(4):
        from_ = [["slots"], [">hn"], [">ho"], [">hn"]][q]
        plan.add(f"hy{q}", lambda q=q: hidden_pass(q), from_, 0.1, "y", 0.15)

    experts = [(((x + j) % 4) * 16 + y * 4 + h).astype(F32) for j in range(4)]
    group_sum = (iota((16, TOK), 1) // 8 == iota((16, TOK), 0)).astype(BF)

    def select(q):
        named = []
        for b in range(4):
            block = s.xb[q, b, FEAT:XROWS].astype(F32)[0:8]
            named += [(block == experts[j]).astype(F32) for j in range(4)]
        hit = dot(group_sum, jnp.concatenate(named, axis=0).astype(BF))
        place = jnp.where(hit > 0.5, dot(hit.astype(BF), upper), -1.0)
        want = iota((CAP, TOK), 0).astype(F32)
        for b in range(4):
            for j in range(4):
                row = place[b * 4 + j : b * 4 + j + 1]
                s.pb[q, j * 128 + b * CAP : j * 128 + (b + 1) * CAP, b * TOK : (b + 1) * TOK] = (
                    row == want
                ).astype(BF)
        feats = jnp.concatenate([s.xb[q, b, 0:FEAT] for b in range(4)], axis=1)
        s.xs[q] = dot(feats, s.pb[q], 1, 1).astype(BF)

    def project(q):
        for j in range(4):
            value = dot(s.lt[j], s.xs[q, :, j * TOK : (j + 1) * TOK])
            s.lp[q, 0, j] = value[0:R]
            s.lp[q, 1, j] = value[R : 2 * R]

    def allreduce(name, task, after):
        plan.add(name + "0", task.start, after, 0.1, "core", 0.25)
        plan.add(name + "1", task.outer, [">" + name + "0"], 0.2, "zi", 0.25)
        plan.add(name + "2", task.swap, [">" + name + "1"], 0.2, "zm", 0.25)
        plan.add(name + "3", task.share, [">" + name + "2"], 0.2, "zo", 0.25)
        plan.add(name + "4", task.across, [">" + name + "3"], 0.1, "core", 0.125)
        plan.add(name + "5", task.done, [">" + name + "4"], 0.05)

    low = [
        AllReduce(s.lp.at[q], s.lc.at[q], s.ls.at[q], s.lz.at[q], s.lo.at[q])
        for q in range(4)
    ]
    dlow = [
        AllReduce(s.kp.at[q], s.kc.at[q], s.ks.at[q], s.kz.at[q], s.ko.at[q])
        for q in range(4)
    ]

    def middle(q):
        for copy in hop[q]:
            copy.wait_recv()
        acts = jnp.concatenate([s.ab[q, b] for b in range(4)], axis=1)
        acts = dot(acts, s.pb[q], 1, 1)
        cot = jnp.concatenate([s.hb[q, b] for b in range(4)], axis=1)
        cot = dot(cot, s.pm[...], 1, 1)
        gate = acts[0:HID] + jnp.concatenate(
            [dot(s.wb[j, 1024:1120], s.lo[q, 0, j]) for j in range(4)], axis=1
        )
        up = acts[HID : 2 * HID] + jnp.concatenate(
            [dot(s.wb[j, 1120:1216], s.lo[q, 1, j]) for j in range(4)], axis=1
        )
        sigma = jax.nn.sigmoid(gate)
        s.dg[q, 0:HID] = (cot * up * sigma * (1.0 + gate * (1.0 - sigma))).astype(BF)
        s.dg[q, HID : 2 * HID] = (cot * gate * sigma).astype(BF)
        for j in range(4):
            for half in range(2):
                s.kp[q, half, j] = dot(
                    s.wb[j, 1024 + half * HID : 1120 + half * HID],
                    s.dg[q, half * HID : (half + 1) * HID, j * TOK : (j + 1) * TOK],
                    0,
                    0,
                )

    def sums(q):
        part = dot(s.dg[q], s.pb[q])
        for b in range(4):
            s.gw[q, b] = part[:, b * TOK : (b + 1) * TOK]
            s.gp[q, b] = part[:, b * TOK : (b + 1) * TOK].astype(BF)

    def inputs(q, n):
        delta = []
        for j in range(4):
            lo = n * (FEAT // 2)
            left = jnp.concatenate(
                [s.wb[j, lo : lo + 256], s.wb[j, 512 + lo : 768 + lo]], axis=1
            )
            back = jnp.concatenate([s.ko[q, 0, j], s.ko[q, 1, j]], axis=0)
            delta.append(dot(left, back).astype(BF))
        part = dot(jnp.concatenate(delta, axis=1), s.pb[q])
        for b in range(4):
            s.dw[n, q, b] = part[:, b * TOK : (b + 1) * TOK]
            s.dp[n, q, b] = part[:, b * TOK : (b + 1) * TOK].astype(BF)

    def keep(task, wide, narrow):
        total = task.finish()
        wide[...] = total
        narrow[...] = total.astype(BF)

    d_halves = rows(0, 128), rows(128, 256)
    for q in (0, 1, 3, 2):
        plan.add(f"sel{q}", lambda q=q: select(q), ["tab", f"xy{q}2"], 0.5)
        plan.add(f"prj{q}", lambda q=q: project(q), ["lt", f"sel{q}"], 0.3)
        allreduce(f"lo{q}", low[q], [f"prj{q}"])
        plan.add(f"mid{q}", lambda q=q: middle(q), [f"lo{q}5", f"ay{q}2", f">hy{q}"], 0.5)
        allreduce(f"dl{q}", dlow[q], [f"mid{q}"])
        plan.add(f"sum{q}", lambda q=q: sums(q), [f"mid{q}"], 0.2)
        task = Direct(
            "dy",
            lambda i, q=q: s.gp.at[q, i],
            lambda i, q=q: s.gw.at[q, i],
            lambda i, q=q: s.gf.at[q, i],
        )
        direct(
            f"gy{q}", task, "y", 0.24, [f"sum{q}"],
            lambda q=q, task=task: keep(task, s.gv.at[q], s.gq.at[q]), 0.15,
        )
        for n in range(2):
            plan.add(f"inp{q}{n}", lambda q=q, n=n: inputs(q, n), [f"dl{q}5"], 0.25)
            task = Scatter(
                "dy",
                lambda i, q=q, n=n: s.dp.at[n, q, i],
                lambda i, q=q, n=n: s.dw.at[n, q, i],
                lambda i, q=q, n=n: s.dr.at[n, q, i],
                lambda i, q=q, n=n: s.df.at[n, q, i],
                *d_halves,
            )
            scatter(
                f"d{n}y{q}", task, "y", 0.125, [f"inp{q}{n}"],
                lambda q=q, n=n, task=task: keep(task, s.dv.at[n, q], s.dq.at[n, q]), 0.15,
            )

    kept = {}

    def ring_h(name, task, size, last, cost):
        along = name[:-1] + "y"
        near = [along + f"{q}2" for q in (1, 3)]
        plan.add(name + "0", task.start, [along + "22"], 0.1, "z", size / 2)
        plan.add(name + "1", task.mid, [">" + name + "0"] + near, cost, "z", size)
        plan.add(name + "2", last, [">" + name + "1", along + "02"], cost)

    gh = Scatter(
        "dh",
        lambda i: s.gq.at[i],
        lambda i: s.gv.at[i],
        lambda i: s.hr.at[i],
        lambda i: s.hf.at[i],
        *a_halves,
    )

    def token_sums():
        total = gh.finish().astype(BF)
        s.gs[0, l, c] = total[0:HID]
        s.gs[1, l, c] = total[HID : 2 * HID]
        kept["gs"] = [
            send(s.gs.at[:, l, c], s.gs.at[:, l, c], dl=i) for i in (1, 2, 3)
        ]

    def token_sums_across():
        for copy in kept["gs"]:
            copy.wait_recv()
        kept["gc"] = send(s.gs.at[:, :, c], s.gs.at[:, :, c], dc=1)

    ring_h("gh", gh, 0.375, lambda: None, 0.1)
    plan.add("gs0", token_sums, ["gh2"], 0.2, "z", 0.375)
    plan.add("gs1", token_sums_across, [">gs0"], 0.1, "core", 0.2)

    def base_grads(n):
        if n == 0:
            kept["gc"].wait_recv()
        lo = n * (FF // 2)
        whole = [s.gs[half].reshape(FF, TOK)[lo : lo + FF // 2] for half in range(2)]
        for place in range(4):
            piece = s.xb[0, 0, place * 128 : (place + 1) * 128]
            both = jnp.concatenate(
                [dot(piece, whole[half], 1, 1).reshape(16, 8, FF // 2) for half in range(2)],
                axis=1,
            ).reshape(4, 4, 16, FF // 2)
            s.bw[n, place] = both
            s.bg[n, place] = both.astype(BF)

    def base_out(n, task):
        grad = task.finish()
        lo = n * (FF // 2)
        o_gb[:, lo : lo + FF // 2] = grad[0:8]
        o_ub[:, lo : lo + FF // 2] = grad[8:16]

    for n in range(2):
        plan.add(f"bas{n}", lambda n=n: base_grads(n), [">gs1"] + ["bas0"] * n, 0.35)
        bx = Scatter(
            "dx",
            lambda i, n=n: s.bg.at[n, (x + i) % 4],
            lambda i, n=n: s.bw.at[n, (x + i) % 4],
            lambda i, n=n: s.bxr.at[n, i],
            lambda i, n=n: s.bxf.at[n, i],
            rows(0, 2),
            rows(2, 4),
        )
        by = Direct(
            "dy",
            lambda i, n=n: s.by.at[n, (y + i) % 4],
            lambda i, n=n: s.byw.at[n, (y + i) % 4],
            lambda i, n=n: s.byf.at[n, i],
        )
        bz = Direct(
            "dh",
            lambda i, n=n: s.bz.at[n, (h + i) % 4],
            lambda i, n=n: s.bzw.at[n, (h + i) % 4],
            lambda i, n=n: s.bzf.at[n, i],
        )
        scatter(
            f"bx{n}", bx, "x", 0.375, [f"bas{n}"],
            lambda n=n, bx=bx: keep(bx, s.byw.at[n], s.by.at[n]), 0.2,
        )
        direct(
            f"by{n}", by, "y", 0.14, [f"bx{n}2"],
            lambda n=n, by=by: keep(by, s.bzw.at[n], s.bz.at[n]), 0.1,
        )
        direct(f"bz{n}", bz, "z", 0.25, [f"by{n}2"], lambda n=n, bz=bz: base_out(n, bz), 0.1)

    def weight_grads():
        for j in range(4):
            slots = jnp.concatenate(
                [s.xs[q, :, j * TOK : (j + 1) * TOK] for q in range(4)], axis=1
            )
            for half in range(2):
                back = jnp.concatenate([s.ko[q, half, j] for q in range(4)], axis=1)
                left = dot(slots, back, 1, 1)
                s.ww[j, half * 512 : (half + 1) * 512] = left
                s.wg[j, half * 512 : (half + 1) * 512] = left.astype(BF)
                lows = jnp.concatenate([s.lo[q, half, j] for q in range(4)], axis=1)
                dgs = jnp.concatenate(
                    [
                        s.dg[q, half * HID : (half + 1) * HID, j * TOK : (j + 1) * TOK]
                        for q in range(4)
                    ],
                    axis=1,
                )
                right = dot(dgs, lows, 1, 1)
                s.ww[j, 1024 + half * HID : 1120 + half * HID] = right
                s.wg[j, 1024 + half * HID : 1120 + half * HID] = right.astype(BF)

    wgx = Scatter(
        "dx",
        lambda i: s.wg.at[i],
        lambda i: s.ww.at[i],
        lambda i: s.wr.at[i],
        lambda i: s.wf.at[i],
        *w_halves,
    )

    def weight_out():
        grads = wgx.finish()
        o_gl[0] = grads[0:512]
        o_ul[0] = grads[512:1024]
        o_gr[0] = grads[1024:1120]
        o_ur[0] = grads[1120:1216]

    plan.add("wgr", weight_grads, [f"dl{q}5" for q in range(4)], 0.8)
    scatter("wgx", wgx, "x", 0.6, ["wgr"], weight_out, 0.3)

    dh = [
        Scatter(
            "dh",
            lambda i, n=n: s.dq.at[n, i],
            lambda i, n=n: s.dv.at[n, i],
            lambda i, n=n: s.er.at[n, i],
            lambda i, n=n: s.ef.at[n, i],
            *d_halves,
        )
        for n in range(2)
    ]

    def base_input(n):
        whole = [s.gs[half].reshape(FF, TOK) for half in range(2)]
        lo = n * (FEAT // 2)
        part = dot(gbase[lo : lo + 256], whole[0]) + dot(ubase[lo : lo + 256], whole[1])
        s.dv[n, 0] = s.dv[n, 0] + part

    def token_out(n):
        lo = n * (FEAT // 2)
        o_tok[:, lo : lo + 256] = dh[n].finish().T.astype(BF)

    for n in range(2):
        plan.add(f"bin{n}", lambda n=n: base_input(n), [">gs1", "bas0", f"d{n}y02"], 0.3)
        ring_h(f"d{n}h", dh[n], 0.5, lambda: None, 0.2)
        plan.add(f"tok{n}", lambda n=n: token_out(n), [f"d{n}h2", f"bin{n}"], 0.2)

    for name in plan.order():
        plan.steps[name][0]()
    for copy in started:
        copy.wait_send()


def hand_on(*refs):
    for given, taken in zip(refs[:7], refs[7:]):
        taken[...] = given[...]


def local(tokens, routes, hidden, gbase, ubase, gleft, uleft, gright, uright):
    vmem = pl.BlockSpec(memory_space=pltpu.VMEM)
    anywhere = pl.BlockSpec(memory_space=pl.ANY)
    shapes = [
        ((TOK, FEAT), BF),
        ((8, FF), F32),
        ((8, FF), F32),
        ((1, FEAT, R), F32),
        ((1, FEAT, R), F32),
        ((1, HID, R), F32),
        ((1, HID, R), F32),
    ]
    outs = pl.pallas_call(
        kernel,
        out_shape=[jax.ShapeDtypeStruct(*shape) for shape in shapes],
        in_specs=[vmem] * 2 + [anywhere] * 7,
        out_specs=[vmem] * 7,
        scratch_shapes=[pltpu.VMEM(*shape) for shape in SCRATCH.values()]
        + [pltpu.SemaphoreType.DMA((SEMS,)), pltpu.SemaphoreType.DMA((SEMS,)), pltpu.SemaphoreType.DMA((7,))],
        compiler_params=pltpu.CompilerParams(
            collective_id=0, has_side_effects=True, vmem_limit_bytes=60 * 1024 * 1024
        ),
    )(
        tokens,
        routes.T,
        jnp.transpose(hidden, (1, 2, 0)),
        gbase,
        ubase,
        gleft,
        uleft,
        jnp.swapaxes(gright, 1, 2),
        jnp.swapaxes(uright, 1, 2),
    )
    outs = pl.pallas_call(
        hand_on,
        out_shape=[jax.ShapeDtypeStruct(*shape) for shape in shapes],
        in_specs=[vmem] * 7,
        out_specs=[vmem] * 7,
    )(*outs)
    return (*outs[:5], jnp.swapaxes(outs[5], 1, 2), jnp.swapaxes(outs[6], 1, 2))


def solution(mesh):
    return jax.shard_map(
        local,
        mesh=mesh,
        in_specs=(
            P("expert", "fsdp"),
            P("expert", None),
            P("expert", None, "fsdp"),
            P("fsdp", None),
            P("fsdp", None),
            P("expert", "fsdp", None),
            P("expert", "fsdp", None),
            P("expert", None, "fsdp"),
            P("expert", None, "fsdp"),
        ),
        out_specs=(
            P("expert", "fsdp"),
            P(("fsdp", "expert"), None),
            P(("fsdp", "expert"), None),
            P("expert", "fsdp", None),
            P("expert", "fsdp", None),
            P("expert", None, "fsdp"),
            P("expert", None, "fsdp"),
        ),
        check_vma=False,
    )
```

```python
import types

import jax
import jax.numpy as jnp
from jax import lax
from jax.experimental import pallas as pl
from jax.experimental.pallas import tpu as pltpu
from jax.sharding import PartitionSpec as P

BF = jnp.bfloat16
F32 = jnp.float32
MESH = pl.DeviceIdType.MESH
TOK = 128
FEAT = 512
HID = 96
FF = 768
R = 128
CAP = 32
XROWS = 528
WROWS = 1216
SEMS = 288


def dot(a, b, ca=1, cb=0):
    return lax.dot_general(a, b, (((ca,), (cb,)), ((), ())), preferred_element_type=F32)


def iota(shape, dim):
    return lax.broadcasted_iota(jnp.int32, shape, dim)


SCRATCH = dict(
    ti=((TOK, FEAT), BF),
    ri=((8, TOK), jnp.int32),
    hi=((8, HID, TOK), BF),
    gi=((FEAT, FF), BF),
    ui=((FEAT, FF), BF),
    xb=((4, 4, XROWS, TOK), BF),
    wb=((4, WROWS, R), BF),
    lt=((4, 2 * R, FEAT), BF),
    ap=((2, 4, 2 * HID, TOK), F32),
    ac=((4, 2 * HID, TOK), F32),
    as_=((4, 2 * HID, TOK), BF),
    az=((3, 2 * HID, TOK), BF),
    ab=((4, 4, 2 * HID, TOK), BF),
    ho=((4, 4, HID, TOK), BF),
    hw=((2, 2, HID, TOK), BF),
    hm=((4, 4, HID, TOK), BF),
    hb=((4, 4, HID, TOK), BF),
    pm=((4 * TOK, 4 * TOK), BF),
    pb=((4, 4 * TOK, 4 * TOK), BF),
    xs=((4, FEAT, 4 * TOK), BF),
    lp=((4, 2, 4, R, TOK), F32),
    lc=((4, 4, R, TOK), F32),
    ls=((4, 4, R, TOK), BF),
    lz=((4, 2, 4, R, TOK), BF),
    lo=((4, 2, 4, R, TOK), BF),
    kp=((4, 2, 4, R, TOK), F32),
    kc=((4, 4, R, TOK), F32),
    ks=((4, 4, R, TOK), BF),
    kz=((4, 2, 4, R, TOK), BF),
    ko=((4, 2, 4, R, TOK), BF),
    dg=((4, 2 * HID, 4 * TOK), BF),
    gp=((4, 4, 2 * HID, TOK), BF),
    gw=((4, 4, 2 * HID, TOK), F32),
    gf=((4, 3, 2 * HID, TOK), BF),
    gs=((4, 2, 4, 2 * HID, TOK), BF),
    dp=((2, 4, 4, FEAT // 2, TOK), BF),
    dw=((2, 4, 4, FEAT // 2, TOK), F32),
    dr=((2, 4, 2, FEAT // 4, TOK), BF),
    df=((2, 4, 2, FEAT // 2, TOK), BF),
    dq=((2, 4, FEAT // 2, TOK), BF),
    dv=((2, 4, FEAT // 2, TOK), F32),
    er=((2, 2, FEAT // 4, TOK), BF),
    ef=((2, 2, FEAT // 2, TOK), BF),
    wg=((4, WROWS, R), BF),
    ww=((4, WROWS, R), F32),
    wr=((2, WROWS // 2, R), BF),
    wf=((2, WROWS, R), BF),
    bg=((2, 4, 4, 4, 16, FF // 2), BF),
    bw=((2, 4, 4, 4, 16, FF // 2), F32),
    bxr=((2, 2, 2, 4, 16, FF // 2), BF),
    bxf=((2, 2, 4, 4, 16, FF // 2), BF),
    by=((2, 4, 4, 16, FF // 2), BF),
    byw=((2, 4, 4, 16, FF // 2), F32),
    byf=((2, 3, 4, 16, FF // 2), BF),
    bz=((2, 4, 16, FF // 2), BF),
    bzw=((2, 4, 16, FF // 2), F32),
    bzr=((2, 2, 16, FF // 2), BF),
    bzf=((2, 2, 16, FF // 2), BF),
)


ORDER = (
    0, 20, 15, 16, 21, 22, 3, 4, 40, 17, 5, 48, 1, 9, 18, 19, 49, 50, 6, 51, 23, 24, 10, 11, 108, 109, 110, 2, 12,
    111, 52, 39, 44, 13, 27, 41, 25, 53, 33, 14, 138, 139, 140, 30, 141, 112, 31, 7, 8, 42, 45, 78, 79, 80, 47, 81,
    28, 26, 54, 36, 142, 113, 34, 55, 29, 56, 57, 63, 64, 43, 114, 82, 65, 58, 143, 37, 35, 115, 116, 123, 124, 117,
    118, 46, 66, 144, 83, 59, 32, 125, 38, 145, 146, 147, 153, 154, 67, 119, 148, 84, 60, 85, 126, 86, 87, 93, 94,
    155, 120, 149, 88, 61, 127, 95, 156, 121, 150, 89, 62, 74, 122, 130, 134, 131, 157, 75, 96, 151, 135, 90, 128,
    70, 71, 152, 160, 161, 164, 165, 68, 158, 97, 136, 162, 91, 166, 92, 100, 101, 129, 137, 159, 132, 69, 98, 163,
    190, 104, 105, 167, 194, 102, 99, 168, 169, 177, 178, 133, 103, 106, 191, 186, 170, 187, 179, 107, 195, 171,
    172, 180, 181, 76, 188, 173, 174, 72, 182, 183, 175, 184, 77, 196, 197, 73, 192, 193, 176, 189, 185,
)


class Plan:
    def __init__(self):
        self.steps = {}

    def add(self, name, run, after=(), cost=0.1, link=None, size=0.0):
        assert name not in self.steps
        self.steps[name] = (run, tuple(after), cost, link, size)

    def order(self):
        names, done = list(self.steps), set()
        assert sorted(ORDER) == list(range(len(names)))
        for place in ORDER:
            assert all(dep.lstrip(">") in done for dep in self.steps[names[place]][1])
            done.add(names[place])
        return [names[place] for place in ORDER]


def kernel(*refs):
    (tokens_in, routes_in, hidden_in, gbase_in, ubase_in, gleft, uleft, gright, uright) = refs[:9]
    (o_tok, o_gb, o_ub, o_gl, o_ul, o_gr, o_ur) = refs[9:16]
    s = types.SimpleNamespace(**dict(zip(SCRATCH, refs[16 : 16 + len(SCRATCH)])))
    send_sem, recv_sem, read_sem = refs[16 + len(SCRATCH) :]
    tokens, routes, hidden, gbase, ubase = s.ti, s.ri, s.hi, s.gi, s.ui

    e = lax.axis_index("expert")
    f = lax.axis_index("fsdp")
    x, y, h = e // 16, (e // 4) % 4, e % 4
    l, c = f // 2, f % 2

    def at(dx=0, dy=0, dh=0, dl=0, dc=0):
        return (
            ((x + dx) % 4) * 16 + ((y + dy) % 4) * 4 + (h + dh) % 4,
            ((l + dl) % 4) * 2 + (c + dc) % 2,
        )

    peers = [dict(dx=1), dict(dx=3), dict(dy=1), dict(dy=2), dict(dy=3), dict(dh=1), dict(dh=3)]
    peers += [dict(dl=1), dict(dl=2), dict(dl=3), dict(dc=1)]
    barrier = pltpu.get_barrier_semaphore()
    for peer in peers:
        pl.semaphore_signal(barrier, inc=1, device_id=at(**peer), device_id_type=MESH)

    reads = [
        pltpu.make_async_copy(src, dst, read_sem.at[n])
        for n, (src, dst) in enumerate(
            [
                (gleft.at[0], s.wb.at[0, 0:512]),
                (uleft.at[0], s.wb.at[0, 512:1024]),
                (gright.at[0], s.wb.at[0, 1024:1120]),
                (uright.at[0], s.wb.at[0, 1120:1216]),
                (gbase_in, gbase),
                (ubase_in, ubase),
                (hidden_in, hidden),
                (tokens_in, tokens),
                (routes_in, routes),
            ]
        )
    ]
    for read in reads[::-1]:
        read.start()

    started = []

    class Copy:
        def __init__(self, src, dst, here, there, where):
            self.src, self.dst, self.here, self.there, self.where = src, dst, here, there, where
            self.n = len(started)
            started.append(self)
            self.run(here, lambda copy: copy.start())

        def run(self, when, act):
            def go():
                act(
                    pltpu.make_async_remote_copy(
                        src_ref=self.src,
                        dst_ref=self.dst,
                        send_sem=send_sem.at[self.n],
                        recv_sem=recv_sem.at[self.n],
                        device_id=at(**self.where),
                        device_id_type=MESH,
                    )
                )

            if when is None:
                go()
            else:
                pl.when(when)(go)

        def wait_recv(self):
            self.run(self.there, lambda copy: copy.wait_recv())

        def wait_send(self):
            self.run(self.here, lambda copy: copy.wait_send())

    def send(src, dst, here=None, there=None, **where):
        return Copy(src, dst, here, there, where)

    edge, inner = (l == 0) | (l == 3), (l == 1) | (l == 2)

    class Gather:
        def __init__(self, axis, buf, first, second):
            self.axis, self.buf, self.first, self.second = axis, buf, first, second

        def start(self):
            self.right = send(self.buf(0), self.buf(3), **{self.axis: 1})
            self.left = send(self.buf(0), self.buf(1), **{self.axis: 3})

        def mid(self):
            self.right.wait_recv()
            self.far_right = send(self.first(self.buf(3)), self.first(self.buf(2)), **{self.axis: 1})
            self.left.wait_recv()
            self.far_left = send(self.second(self.buf(1)), self.second(self.buf(2)), **{self.axis: 3})

        def finish(self):
            self.far_right.wait_recv()
            self.far_left.wait_recv()

    class Scatter:
        def __init__(self, axis, part, wide, relay, full, first, second):
            self.axis, self.part, self.wide, self.relay, self.full = axis, part, wide, relay, full
            self.first, self.second = first, second

        def start(self):
            self.a = send(self.first(self.part(2)), self.relay(0), **{self.axis: 1})
            self.b = send(self.second(self.part(2)), self.relay(1), **{self.axis: 3})

        def mid(self):
            for copy, half, i in ((self.a, self.first, 1), (self.b, self.second, 3)):
                copy.wait_recv()
                lane = self.relay(i // 2)[...].astype(F32)
                half(self.part(i))[...] = (half(self.wide(i))[...] + lane).astype(BF)
            self.right = send(self.part(1), self.full(0), **{self.axis: 1})
            self.left = send(self.part(3), self.full(1), **{self.axis: 3})

        def finish(self):
            self.right.wait_recv()
            self.left.wait_recv()
            return (
                self.wide(0)[...]
                + self.full(0)[...].astype(F32)
                + self.full(1)[...].astype(F32)
            )

    class Direct:
        def __init__(self, axis, part, wide, full):
            self.axis, self.part, self.wide, self.full = axis, part, wide, full

        def start(self):
            self.copies = [
                send(self.part(i), self.full(i - 1), **{self.axis: i}) for i in (1, 3, 2)
            ]

        def finish(self):
            total = self.wide(0)[...]
            for i, copy in zip((1, 3, 2), self.copies):
                copy.wait_recv()
                total = total + self.full(i - 1)[...].astype(F32)
            return total

    class Reduce:
        def __init__(self, parts, core, sums, lands):
            self.parts, self.core, self.sums, self.lands = parts, core, sums, lands

        def start(self):
            self.pair = send(self.parts.at[1 - c], self.core, dc=1)

        def mid(self):
            self.pair.wait_recv()
            total = self.parts[c] + self.core[...]
            self.parts[c] = total
            self.sums[...] = total.astype(BF)
            self.hops = [
                send(self.sums.at[(l + i) % 4], self.lands.at[i - 1], dl=i) for i in (1, 2, 3)
            ]

        def finish(self):
            total = self.parts[c, l]
            for i, hop in enumerate(self.hops):
                hop.wait_recv()
                total = total + self.lands[i].astype(F32)
            return total.astype(BF)

    class AllReduce:
        def __init__(self, parts, core, sums, lands, out):
            self.parts, self.core, self.sums, self.lands, self.out = parts, core, sums, lands, out

        def start(self):
            self.pair = send(self.parts.at[1 - c], self.core, dc=1)

        def outer(self):
            self.pair.wait_recv()
            total = self.parts[c] + self.core[...]
            self.parts[c] = total

            @pl.when(edge)
            def _():
                self.sums[...] = total.astype(BF)

            self.up = send(self.sums, self.lands.at[0], edge, inner, dl=1 - 2 * (l % 2))

        def swap(self):
            self.up.wait_recv()

            @pl.when(inner)
            def _():
                total = self.parts[c] + self.lands[0].astype(F32)
                self.parts[c] = total
                self.sums[...] = total.astype(BF)

            self.over = send(self.sums, self.lands.at[1], inner, inner, dl=3 - 2 * l)

        def share(self):
            self.over.wait_recv()

            @pl.when(inner)
            def _():
                self.out[c] = (self.parts[c] + self.lands[1].astype(F32)).astype(BF)

            self.down = send(self.out.at[c], self.out.at[c], inner, edge, dl=1 - 2 * (l % 2))
            self.inner_pair = send(self.out.at[c], self.out.at[c], inner, inner, dc=1)

        def across(self):
            self.down.wait_recv()
            self.edge_pair = send(self.out.at[c], self.out.at[c], edge, edge, dc=1)

        def done(self):
            self.inner_pair.wait_recv()
            self.edge_pair.wait_recv()

    class Share:
        def __init__(self, out, task):
            self.out, self.task = out, task

        def start(self):
            self.out[c, l] = self.task.finish().astype(BF)
            own = self.out.at[c, l]
            self.up = send(own, own, edge, inner, dl=1 - 2 * (l % 2))

        def swap(self):
            self.up.wait_recv()
            pair = self.out.at[c, pl.ds(2 * (l // 2), 2)]
            self.over = send(pair, pair, inner, inner, dl=3 - 2 * l)

        def back(self):
            self.over.wait_recv()
            others = self.out.at[c, pl.ds(jnp.maximum(2 - l, 0) % 2, 3)]
            self.down = send(others, others, inner, edge, dl=1 - 2 * (l % 2))
            self.inner_pair = send(self.out.at[c], self.out.at[c], inner, inner, dc=1)

        def across(self):
            self.down.wait_recv()
            self.edge_pair = send(self.out.at[c], self.out.at[c], edge, edge, dc=1)

        def done(self):
            self.inner_pair.wait_recv()
            self.edge_pair.wait_recv()

    def rows(lo, hi):
        return lambda ref: ref.at[lo:hi]

    reads[7].wait()
    reads[8].wait()
    routes_t = routes[...].astype(F32)
    s.xb[0, 0, 0:FEAT] = tokens[...].T
    s.xb[0, 0, FEAT:XROWS] = jnp.concatenate(
        [routes_t, jnp.zeros((8, TOK), F32)], axis=0
    ).astype(BF)
    pl.semaphore_wait(barrier, len(peers))

    plan = Plan()

    upper = (iota((TOK, TOK), 0) < iota((TOK, TOK), 1)).astype(BF)

    def own_weights():
        for read in reads[0:4]:
            read.wait()

    def own_partials():
        reads[4].wait()
        reads[5].wait()
        for half, base in enumerate((gbase, ubase)):
            part = dot(tokens[...], base[...]).T
            for place in range(4):
                for core in range(2):
                    lo = (place * 2 + core) * HID
                    s.ap[core, place, half * HID : (half + 1) * HID] = part[lo : lo + HID]

    def own_slots():
        reads[6].wait()
        ranks = iota((64, TOK), 0)
        names = (
            ((x + ranks % 4) % 4) * 16 + ((y + (ranks // 4) % 4) % 4) * 4 + (h + ranks // 16) % 4
        ).astype(F32)
        chosen = [(names == routes_t[k : k + 1]).astype(F32) for k in range(8)]
        order = dot(sum(chosen).astype(BF), upper) + ranks.astype(F32) * CAP
        slot = [jnp.sum(chosen[k] * order, axis=0, keepdims=True) for k in range(8)]
        hid_t = jnp.concatenate([hidden[k] for k in range(8)], axis=1)
        for place in range(16):
            want = (iota((TOK, TOK), 0) + place * TOK).astype(F32)
            pick = jnp.concatenate([(slot[k] == want).astype(BF) for k in range(8)], axis=1)
            s.ho[place // 4, place % 4] = dot(hid_t, pick, 1, 1).astype(BF)
        s.hb[0, 0] = s.ho[0, 0]

    def tables():
        r4, c4 = iota((512, 512), 0), iota((512, 512), 1)
        s.pm[...] = (
            (r4 // 128 == (c4 // 32) % 4) & ((r4 // 32) % 4 == c4 // 128) & (r4 % 32 == c4 % 32)
        ).astype(BF)
        s.pb[...] = jnp.zeros_like(s.pb)

    def gather(name, task, link, size, after=()):
        plan.add(name + "0", task.start, after, 0.1, link, size)
        plan.add(name + "1", task.mid, [">" + name + "0"], 0.1, link, size / 2)
        plan.add(name + "2", task.finish, [">" + name + "1"], 0.05)

    def scatter(name, task, link, size, after, last, cost=0.3, late=()):
        plan.add(name + "0", task.start, after, 0.1, link, size / 2)
        plan.add(name + "1", task.mid, [">" + name + "0"] + list(after), 0.15, link, size)
        plan.add(name + "2", last, [">" + name + "1"] + list(late), cost)

    def direct(name, task, link, size, after, last, cost=0.2):
        plan.add(name + "0", task.start, after, 0.1, link, size)
        plan.add(name + "2", last, [">" + name + "0"], cost)

    x_halves = rows(0, 256), rows(256, XROWS)
    gather("xh", Gather("dh", lambda i: s.xb.at[i, 0], *x_halves), "z", 1.0)
    for q in (0, 1, 3, 2):
        task = Gather("dy", lambda i, q=q: s.xb.at[q, i], *x_halves)
        gather(f"xy{q}", task, "y", 0.25, [[], ["xh1"], ["xh2"], ["xh1"]][q])
    plan.add("wts", own_weights, [], 0.2)
    w_halves = rows(0, WROWS // 2), rows(WROWS // 2, WROWS)
    gather("wx", Gather("dx", lambda i: s.wb.at[i], *w_halves), "x", 0.6, ["wts"])

    def turn():
        for j in range(4):
            s.lt[j, 0:R] = s.wb[j, 0:512].T
            s.lt[j, R : 2 * R] = s.wb[j, 512:1024].T

    plan.add("lt", turn, ["wx2"], 0.5)

    act = Reduce(s.ap, s.ac, s.as_, s.az)

    def own_act():
        s.ab[0, 0] = act.finish()

    plan.add("actp", own_partials, [], 0.8)
    plan.add("act0", act.start, ["actp"], 0.1, "core", 0.375)
    plan.add("act1", act.mid, [">act0"], 0.3, "z", 0.375)
    plan.add("act2", own_act, [">act1"], 0.2)
    a_halves = rows(0, HID), rows(HID, 2 * HID)
    gather("ah", Gather("dh", lambda i: s.ab.at[i, 0], *a_halves), "z", 0.375, ["act2"])
    for q in (0, 1, 3, 2):
        task = Gather("dy", lambda i, q=q: s.ab.at[q, i], *a_halves)
        gather(f"ay{q}", task, "y", 0.1, [["act2"], ["ah1"], ["ah2"], ["ah1"]][q])

    hop = {}

    def hidden_near():
        hop["near"] = [send(s.ho.at[i], s.hm.at[4 - i], dh=i) for i in (1, 3)]

    def hidden_far():
        hop["far"] = [
            send(s.ho.at[2, 0:2], s.hw.at[0], dh=1),
            send(s.ho.at[2, 2:4], s.hw.at[1], dh=3),
        ]

    def hidden_on():
        hop["on"] = []
        for n, copy in enumerate(hop["far"]):
            copy.wait_recv()
            hop["on"].append(
                send(s.hw.at[n], s.hm.at[2, 2 * n : 2 * n + 2], dh=(1, 3)[n])
            )

    def hidden_pass(q):
        if q in (1, 3):
            hop["near"][{3: 0, 1: 1}[q]].wait_recv()
        elif q == 2:
            for copy in hop["on"]:
                copy.wait_recv()
        held = s.ho if q == 0 else s.hm
        if q:
            s.hb[q, 0] = s.hm[q, 0]
        hop[q] = [send(held.at[q, j], s.hb.at[q, 4 - j], dy=j) for j in (1, 2, 3)]

    plan.add("slots", own_slots, [], 1.5)
    plan.add("tab", tables, [], 0.4)
    plan.add("hn", hidden_near, ["slots", "xh1"], 0.1, "z", 0.75)
    plan.add("hf", hidden_far, ["slots", "xh1"], 0.1, "z", 0.375)
    plan.add("ho", hidden_on, [">hf"], 0.1, "z", 0.375)
    for q in range(4):
        from_ = [["slots"], [">hn"], [">ho"], [">hn"]][q]
        plan.add(f"hy{q}", lambda q=q: hidden_pass(q), from_, 0.1, "y", 0.15)

    experts = [(((x + j) % 4) * 16 + y * 4 + h).astype(F32) for j in range(4)]
    group_sum = (iota((16, TOK), 1) // 8 == iota((16, TOK), 0)).astype(BF)

    def select(q):
        named = []
        for b in range(4):
            block = s.xb[q, b, FEAT:XROWS].astype(F32)[0:8]
            named += [(block == experts[j]).astype(F32) for j in range(4)]
        hit = dot(group_sum, jnp.concatenate(named, axis=0).astype(BF))
        place = jnp.where(hit > 0.5, dot(hit.astype(BF), upper), -1.0)
        want = iota((CAP, TOK), 0).astype(F32)
        for b in range(4):
            for j in range(4):
                row = place[b * 4 + j : b * 4 + j + 1]
                s.pb[q, j * 128 + b * CAP : j * 128 + (b + 1) * CAP, b * TOK : (b + 1) * TOK] = (
                    row == want
                ).astype(BF)
        feats = jnp.concatenate([s.xb[q, b, 0:FEAT] for b in range(4)], axis=1)
        s.xs[q] = dot(feats, s.pb[q], 1, 1).astype(BF)

    def project(q):
        for j in range(4):
            value = dot(s.lt[j], s.xs[q, :, j * TOK : (j + 1) * TOK])
            s.lp[q, 0, j] = value[0:R]
            s.lp[q, 1, j] = value[R : 2 * R]

    def allreduce(name, task, after):
        plan.add(name + "0", task.start, after, 0.1, "core", 0.25)
        plan.add(name + "1", task.outer, [">" + name + "0"], 0.2, "zi", 0.25)
        plan.add(name + "2", task.swap, [">" + name + "1"], 0.2, "zm", 0.25)
        plan.add(name + "3", task.share, [">" + name + "2"], 0.2, "zo", 0.25)
        plan.add(name + "4", task.across, [">" + name + "3"], 0.1, "core", 0.125)
        plan.add(name + "5", task.done, [">" + name + "4"], 0.05)

    low = [
        AllReduce(s.lp.at[q], s.lc.at[q], s.ls.at[q], s.lz.at[q], s.lo.at[q])
        for q in range(4)
    ]
    dlow = [
        AllReduce(s.kp.at[q], s.kc.at[q], s.ks.at[q], s.kz.at[q], s.ko.at[q])
        for q in range(4)
    ]

    def middle(q):
        for copy in hop[q]:
            copy.wait_recv()
        acts = jnp.concatenate([s.ab[q, b] for b in range(4)], axis=1)
        acts = dot(acts, s.pb[q], 1, 1)
        cot = jnp.concatenate([s.hb[q, b] for b in range(4)], axis=1)
        cot = dot(cot, s.pm[...], 1, 1)
        gate = acts[0:HID] + jnp.concatenate(
            [dot(s.wb[j, 1024:1120], s.lo[q, 0, j]) for j in range(4)], axis=1
        )
        up = acts[HID : 2 * HID] + jnp.concatenate(
            [dot(s.wb[j, 1120:1216], s.lo[q, 1, j]) for j in range(4)], axis=1
        )
        sigma = jax.nn.sigmoid(gate)
        s.dg[q, 0:HID] = (cot * up * sigma * (1.0 + gate * (1.0 - sigma))).astype(BF)
        s.dg[q, HID : 2 * HID] = (cot * gate * sigma).astype(BF)
        for j in range(4):
            for half in range(2):
                s.kp[q, half, j] = dot(
                    s.wb[j, 1024 + half * HID : 1120 + half * HID],
                    s.dg[q, half * HID : (half + 1) * HID, j * TOK : (j + 1) * TOK],
                    0,
                    0,
                )

    def sums(q):
        part = dot(s.dg[q], s.pb[q])
        for b in range(4):
            s.gw[q, b] = part[:, b * TOK : (b + 1) * TOK]
            s.gp[q, b] = part[:, b * TOK : (b + 1) * TOK].astype(BF)

    def inputs(q, n):
        delta = []
        for j in range(4):
            lo = n * (FEAT // 2)
            left = jnp.concatenate(
                [s.wb[j, lo : lo + 256], s.wb[j, 512 + lo : 768 + lo]], axis=1
            )
            back = jnp.concatenate([s.ko[q, 0, j], s.ko[q, 1, j]], axis=0)
            delta.append(dot(left, back).astype(BF))
        part = dot(jnp.concatenate(delta, axis=1), s.pb[q])
        for b in range(4):
            s.dw[n, q, b] = part[:, b * TOK : (b + 1) * TOK]
            s.dp[n, q, b] = part[:, b * TOK : (b + 1) * TOK].astype(BF)

    def keep(task, wide, narrow):
        total = task.finish()
        wide[...] = total
        narrow[...] = total.astype(BF)

    def token_sums(q, half, first=0, last=4):
        return [
            s.gs[q, core, place, half * HID : (half + 1) * HID]
            for place in range(first, last)
            for core in range(2)
        ]

    def keep_inputs(q, n, task):
        lo = n * (FEAT // 2)
        total = task.finish()
        for half, base in enumerate((gbase, ubase)):
            total = total + dot(base[lo : lo + 256], jnp.concatenate(token_sums(q, half), axis=0))
        s.dv[n, q] = total
        s.dq[n, q] = total.astype(BF)

    d_halves = rows(0, 128), rows(128, 256)
    for q in (0, 1, 3, 2):
        plan.add(f"sel{q}", lambda q=q: select(q), ["tab", f"xy{q}2"], 0.5)
        plan.add(f"prj{q}", lambda q=q: project(q), ["lt", f"sel{q}"], 0.3)
        allreduce(f"lo{q}", low[q], [f"prj{q}"])
        plan.add(f"mid{q}", lambda q=q: middle(q), [f"lo{q}5", f"ay{q}2", f">hy{q}"], 0.5)
        allreduce(f"dl{q}", dlow[q], [f"mid{q}"])
        plan.add(f"sum{q}", lambda q=q: sums(q), [f"mid{q}"], 0.2)
        task = Direct(
            "dy",
            lambda i, q=q: s.gp.at[q, i],
            lambda i, q=q: s.gw.at[q, i],
            lambda i, q=q: s.gf.at[q, i],
        )
        share = Share(s.gs.at[q], task)
        plan.add(f"gy{q}0", task.start, [f"sum{q}"], 0.1, "y", 0.24)
        plan.add(f"ga{q}0", share.start, [f">gy{q}0"], 0.15, "zi", 0.095)
        plan.add(f"ga{q}1", share.swap, [f">ga{q}0"], 0.1, "zm", 0.19)
        plan.add(f"ga{q}2", share.back, [f">ga{q}1"], 0.1, "zo", 0.28)
        plan.add(f"ga{q}3", share.across, [f">ga{q}2"], 0.1, "core", 0.19)
        plan.add(f"ga{q}4", share.done, [f">ga{q}3"], 0.05)
        for n in range(2):
            plan.add(f"inp{q}{n}", lambda q=q, n=n: inputs(q, n), [f"dl{q}5"], 0.25)
            task = Scatter(
                "dy",
                lambda i, q=q, n=n: s.dp.at[n, q, i],
                lambda i, q=q, n=n: s.dw.at[n, q, i],
                lambda i, q=q, n=n: s.dr.at[n, q, i],
                lambda i, q=q, n=n: s.df.at[n, q, i],
                *d_halves,
            )
            scatter(
                f"d{n}y{q}", task, "y", 0.125, [f"inp{q}{n}"],
                lambda q=q, n=n, task=task: keep_inputs(q, n, task), 0.35, [f"ga{q}4"],
            )


    def ring_h(name, task, size, last, cost):
        along = name[:-1] + "y"
        near = [along + f"{q}2" for q in (1, 3)]
        plan.add(name + "0", task.start, [along + "22"], 0.1, "z", size / 2)
        plan.add(name + "1", task.mid, [">" + name + "0"] + near, cost, "z", size)
        plan.add(name + "2", last, [">" + name + "1", along + "02"], cost)

    def base_grads(n):
        whole = [
            jnp.concatenate(
                [
                    jnp.concatenate(token_sums(q, half, 2 * n, 2 * n + 2), axis=0)
                    for q in range(4)
                ],
                axis=1,
            )
            for half in range(2)
        ]
        for place in range(4):
            piece = jnp.concatenate(
                [s.xb[q, 0, place * 128 : (place + 1) * 128] for q in range(4)], axis=1
            )
            both = jnp.concatenate(
                [dot(piece, whole[half], 1, 1).reshape(16, 8, FF // 2) for half in range(2)],
                axis=1,
            ).reshape(4, 4, 16, FF // 2)
            if n == 0:
                s.bw[n, place] = both
                s.bg[n, place] = both.astype(BF)
            else:
                s.bw[n, :, place] = both
                s.bg[n, :, place] = both.astype(BF)

    def base_out(n, task):
        grad = task.finish()
        lo = n * (FF // 2)
        o_gb[:, lo : lo + FF // 2] = grad[0:8]
        o_ub[:, lo : lo + FF // 2] = grad[8:16]

    for n in range(2):
        plan.add(f"bas{n}", lambda n=n: base_grads(n), [f"ga{q}4" for q in range(4)], 0.7)
        bx = Scatter(
            ("dx", "dy")[n],
            lambda i, n=n: s.bg.at[n, ((x, y)[n] + i) % 4],
            lambda i, n=n: s.bw.at[n, ((x, y)[n] + i) % 4],
            lambda i, n=n: s.bxr.at[n, i],
            lambda i, n=n: s.bxf.at[n, i],
            rows(0, 2),
            rows(2, 4),
        )
        by = Direct(
            ("dy", "dx")[n],
            lambda i, n=n: s.by.at[n, ((y, x)[n] + i) % 4],
            lambda i, n=n: s.byw.at[n, ((y, x)[n] + i) % 4],
            lambda i, n=n: s.byf.at[n, i],
        )
        bz = Scatter(
            "dh",
            lambda i, n=n: s.bz.at[n, (h + i) % 4],
            lambda i, n=n: s.bzw.at[n, (h + i) % 4],
            lambda i, n=n: s.bzr.at[n, i, :, 0 : (256, 128)[i]],
            lambda i, n=n: s.bzf.at[n, i],
            lambda ref: ref.at[:, 0:256],
            lambda ref: ref.at[:, 256:384],
        )
        scatter(
            f"bx{n}", bx, ("x", "y")[n], 0.375, [f"bas{n}"],
            lambda n=n, bx=bx: keep(bx, s.byw.at[n], s.by.at[n]), 0.2,
        )
        direct(
            f"by{n}", by, ("y", "x")[n], 0.14, [f"bx{n}2"],
            lambda n=n, by=by: keep(by, s.bzw.at[n], s.bz.at[n]), 0.1,
        )
        scatter(f"bz{n}", bz, "z", 0.1, [f"by{n}2"], lambda n=n, bz=bz: base_out(n, bz), 0.1)

    def weight_grads():
        for j in range(4):
            slots = jnp.concatenate(
                [s.xs[q, :, j * TOK : (j + 1) * TOK] for q in range(4)], axis=1
            )
            for half in range(2):
                back = jnp.concatenate([s.ko[q, half, j] for q in range(4)], axis=1)
                left = dot(slots, back, 1, 1)
                s.ww[j, half * 512 : (half + 1) * 512] = left
                s.wg[j, half * 512 : (half + 1) * 512] = left.astype(BF)
                lows = jnp.concatenate([s.lo[q, half, j] for q in range(4)], axis=1)
                dgs = jnp.concatenate(
                    [
                        s.dg[q, half * HID : (half + 1) * HID, j * TOK : (j + 1) * TOK]
                        for q in range(4)
                    ],
                    axis=1,
                )
                right = dot(dgs, lows, 1, 1)
                s.ww[j, 1024 + half * HID : 1120 + half * HID] = right
                s.wg[j, 1024 + half * HID : 1120 + half * HID] = right.astype(BF)

    wgx = Scatter(
        "dx",
        lambda i: s.wg.at[i],
        lambda i: s.ww.at[i],
        lambda i: s.wr.at[i],
        lambda i: s.wf.at[i],
        *w_halves,
    )

    def weight_out():
        grads = wgx.finish()
        o_gl[0] = grads[0:512]
        o_ul[0] = grads[512:1024]
        o_gr[0] = grads[1024:1120]
        o_ur[0] = grads[1120:1216]

    plan.add("wgr", weight_grads, [f"dl{q}5" for q in range(4)], 0.8)
    scatter("wgx", wgx, "x", 0.6, ["wgr"], weight_out, 0.3)

    dh = [
        Scatter(
            "dh",
            lambda i, n=n: s.dq.at[n, i],
            lambda i, n=n: s.dv.at[n, i],
            lambda i, n=n: s.er.at[n, i],
            lambda i, n=n: s.ef.at[n, i],
            *d_halves,
        )
        for n in range(2)
    ]

    def token_out(n):
        lo = n * (FEAT // 2)
        o_tok[:, lo : lo + 256] = dh[n].finish().T.astype(BF)

    for n in range(2):
        ring_h(f"d{n}h", dh[n], 0.5, lambda: None, 0.2)
        plan.add(f"tok{n}", lambda n=n: token_out(n), [f"d{n}h2"], 0.2)

    for name in plan.order():
        plan.steps[name][0]()
    for copy in started:
        copy.wait_send()


def hand_on(*refs):
    for given, taken in zip(refs[:7], refs[7:]):
        taken[...] = given[...]


def local(tokens, routes, hidden, gbase, ubase, gleft, uleft, gright, uright):
    vmem = pl.BlockSpec(memory_space=pltpu.VMEM)
    anywhere = pl.BlockSpec(memory_space=pl.ANY)
    shapes = [
        ((TOK, FEAT), BF),
        ((8, FF), F32),
        ((8, FF), F32),
        ((1, FEAT, R), F32),
        ((1, FEAT, R), F32),
        ((1, HID, R), F32),
        ((1, HID, R), F32),
    ]
    outs = pl.pallas_call(
        kernel,
        out_shape=[jax.ShapeDtypeStruct(*shape) for shape in shapes],
        in_specs=[anywhere] * 9,
        out_specs=[vmem] * 7,
        scratch_shapes=[pltpu.VMEM(*shape) for shape in SCRATCH.values()]
        + [pltpu.SemaphoreType.DMA((SEMS,)), pltpu.SemaphoreType.DMA((SEMS,)), pltpu.SemaphoreType.DMA((9,))],
        compiler_params=pltpu.CompilerParams(
            collective_id=0, has_side_effects=True, vmem_limit_bytes=60 * 1024 * 1024
        ),
    )(
        tokens,
        routes.T,
        jnp.transpose(hidden, (1, 2, 0)),
        gbase,
        ubase,
        gleft,
        uleft,
        jnp.swapaxes(gright, 1, 2),
        jnp.swapaxes(uright, 1, 2),
    )
    outs = pl.pallas_call(
        hand_on,
        out_shape=[jax.ShapeDtypeStruct(*shape) for shape in shapes],
        in_specs=[vmem] * 7,
        out_specs=[vmem] * 7,
    )(*outs)
    return (*outs[:5], jnp.swapaxes(outs[5], 1, 2), jnp.swapaxes(outs[6], 1, 2))


def solution(mesh):
    return jax.shard_map(
        local,
        mesh=mesh,
        in_specs=(
            P("expert", "fsdp"),
            P("expert", None),
            P("expert", None, "fsdp"),
            P("fsdp", None),
            P("fsdp", None),
            P("expert", "fsdp", None),
            P("expert", "fsdp", None),
            P("expert", None, "fsdp"),
            P("expert", None, "fsdp"),
        ),
        out_specs=(
            P("expert", "fsdp"),
            P(("fsdp", "expert"), None),
            P(("fsdp", "expert"), None),
            P("expert", "fsdp", None),
            P("expert", "fsdp", None),
            P("expert", None, "fsdp"),
            P("expert", None, "fsdp"),
        ),
        check_vma=False,
    )
```

```python
import types

import jax
import jax.numpy as jnp
from jax import lax
from jax.experimental import pallas as pl
from jax.experimental.pallas import tpu as pltpu
from jax.sharding import PartitionSpec as P

BF = jnp.bfloat16
F32 = jnp.float32
MESH = pl.DeviceIdType.MESH
TOK = 128
FEAT = 512
HID = 96
FF = 768
R = 128
CAP = 32
XROWS = 528
WROWS = 1216
SEMS = 288


def dot(a, b, ca=1, cb=0):
    return lax.dot_general(a, b, (((ca,), (cb,)), ((), ())), preferred_element_type=F32)


def iota(shape, dim):
    return lax.broadcasted_iota(jnp.int32, shape, dim)


SCRATCH = dict(
    ti=((TOK, FEAT), BF),
    ri=((8, TOK), jnp.int32),
    hi=((8, HID, TOK), BF),
    gi=((FEAT, FF), BF),
    ui=((FEAT, FF), BF),
    xb=((4, 4, XROWS, TOK), BF),
    wb=((4, WROWS, R), BF),
    lt=((4, 2 * R, FEAT), BF),
    ap=((2, 4, 2 * HID, TOK), F32),
    ac=((4, 2 * HID, TOK), F32),
    as_=((4, 2 * HID, TOK), BF),
    az=((3, 2 * HID, TOK), BF),
    ab=((4, 4, 2 * HID, TOK), BF),
    ho=((4, 4, HID, TOK), BF),
    hw=((2, 2, HID, TOK), BF),
    hm=((4, 4, HID, TOK), BF),
    hb=((4, 4, HID, TOK), BF),
    pm=((4 * TOK, 4 * TOK), BF),
    pb=((4, 4 * TOK, 4 * TOK), BF),
    xs=((4, FEAT, 4 * TOK), BF),
    lp=((4, 2, 4, R, TOK), F32),
    lc=((4, 4, R, TOK), F32),
    ls=((4, 4, R, TOK), BF),
    lz=((4, 2, 4, R, TOK), BF),
    lo=((4, 2, 4, R, TOK), BF),
    kp=((4, 2, 4, R, TOK), F32),
    kc=((4, 4, R, TOK), F32),
    ks=((4, 4, R, TOK), BF),
    kz=((4, 2, 4, R, TOK), BF),
    ko=((4, 2, 4, R, TOK), BF),
    dg=((4, 2 * HID, 4 * TOK), BF),
    gp=((4, 4, 2 * HID, TOK), BF),
    gw=((4, 4, 2 * HID, TOK), F32),
    gf=((4, 3, 2 * HID, TOK), BF),
    gs=((4, 2, 4, 2 * HID, TOK), BF),
    dp=((2, 4, 4, FEAT // 2, TOK), BF),
    dw=((2, 4, 4, FEAT // 2, TOK), F32),
    dr=((2, 4, 2, FEAT // 4, TOK), BF),
    df=((2, 4, 2, FEAT // 2, TOK), BF),
    dq=((2, 4, FEAT // 2, TOK), BF),
    dv=((2, 4, FEAT // 2, TOK), F32),
    er=((2, 2, FEAT // 4, TOK), BF),
    ef=((2, 2, FEAT // 2, TOK), BF),
    wg=((4, WROWS, R), BF),
    ww=((4, WROWS, R), F32),
    wr=((2, WROWS // 2, R), BF),
    wf=((2, WROWS, R), BF),
    bg=((2, 4, 4, 4, 16, FF // 2), BF),
    bw=((2, 4, 4, 4, 16, FF // 2), F32),
    bxr=((2, 2, 2, 4, 16, FF // 2), BF),
    bxf=((2, 2, 4, 4, 16, FF // 2), BF),
    by=((2, 4, 4, 16, FF // 2), BF),
    byw=((2, 4, 4, 16, FF // 2), F32),
    byf=((2, 3, 4, 16, FF // 2), BF),
    bz=((2, 4, 16, FF // 2), BF),
    bzw=((2, 4, 16, FF // 2), F32),
    bzr=((2, 2, 16, FF // 2), BF),
    bzf=((2, 2, 16, FF // 2), BF),
)


ORDER = (
    0, 3, 15, 16, 20, 21, 22, 4, 40, 5, 48, 17, 18, 1, 6, 19, 49, 50, 9, 51, 7, 23, 24, 8, 78, 79, 80, 2, 12, 52,
    81, 39, 44, 41, 13, 10, 25, 30, 53, 14, 31, 138, 82, 139, 11, 33, 140, 141, 27, 32, 108, 109, 34, 110, 42, 111,
    28, 45, 26, 83, 47, 54, 142, 36, 55, 29, 56, 57, 63, 64, 43, 84, 65, 143, 112, 37, 58, 85, 86, 93, 94, 87, 88,
    46, 66, 144, 113, 95, 59, 145, 38, 146, 147, 67, 153, 154, 89, 148, 114, 60, 35, 115, 116, 96, 155, 117, 123,
    124, 90, 149, 118, 97, 61, 156, 91, 150, 119, 125, 62, 92, 100, 101, 74, 75, 157, 104, 70, 105, 126, 71, 76,
    151, 120, 68, 102, 152, 164, 165, 158, 127, 160, 161, 69, 77, 98, 166, 121, 162, 122, 134, 135, 99, 130, 131,
    106, 159, 128, 167, 194, 163, 190, 136, 129, 168, 169, 177, 178, 107, 132, 137, 195, 103, 170, 179, 72, 186,
    187, 133, 191, 171, 172, 180, 181, 196, 197, 73, 188, 173, 174, 182, 183, 192, 193, 175, 189, 184, 176, 185,
)


class Plan:
    def __init__(self):
        self.steps = {}

    def add(self, name, run, after=(), cost=0.1, link=None, size=0.0):
        assert name not in self.steps
        self.steps[name] = (run, tuple(after), cost, link, size)

    def order(self):
        names, done = list(self.steps), set()
        assert sorted(ORDER) == list(range(len(names)))
        for place in ORDER:
            assert all(dep.lstrip(">") in done for dep in self.steps[names[place]][1])
            done.add(names[place])
        return [names[place] for place in ORDER]


def kernel(*refs):
    (tokens_in, routes_in, hidden_in, gbase_in, ubase_in, gleft, uleft, gright, uright) = refs[:9]
    (o_tok, o_gb, o_ub, o_gl, o_ul, o_gr, o_ur) = refs[9:16]
    s = types.SimpleNamespace(**dict(zip(SCRATCH, refs[16 : 16 + len(SCRATCH)])))
    send_sem, recv_sem, read_sem = refs[16 + len(SCRATCH) :]
    tokens, routes, hidden, gbase, ubase = s.ti, s.ri, s.hi, s.gi, s.ui

    e = lax.axis_index("expert")
    f = lax.axis_index("fsdp")
    x, y, h = e // 16, (e // 4) % 4, e % 4
    l, c = f // 2, f % 2

    def at(dx=0, dy=0, dh=0, dl=0, dc=0):
        return (
            ((x + dx) % 4) * 16 + ((y + dy) % 4) * 4 + (h + dh) % 4,
            ((l + dl) % 4) * 2 + (c + dc) % 2,
        )

    peers = [dict(dx=1), dict(dx=3), dict(dy=1), dict(dy=2), dict(dy=3), dict(dh=1), dict(dh=3)]
    peers += [dict(dl=1), dict(dl=2), dict(dl=3), dict(dc=1)]
    barrier = pltpu.get_barrier_semaphore()
    for peer in peers:
        pl.semaphore_signal(barrier, inc=1, device_id=at(**peer), device_id_type=MESH)

    reads = [
        pltpu.make_async_copy(src, dst, read_sem.at[n])
        for n, (src, dst) in enumerate(
            [
                (gleft.at[0], s.wb.at[0, 0:512]),
                (uleft.at[0], s.wb.at[0, 512:1024]),
                (gright.at[0], s.wb.at[0, 1024:1120]),
                (uright.at[0], s.wb.at[0, 1120:1216]),
                (gbase_in, gbase),
                (ubase_in, ubase),
                (hidden_in, hidden),
                (tokens_in, tokens),
                (routes_in, routes),
            ]
        )
    ]
    for read in reads[::-1]:
        read.start()

    started = []

    class Copy:
        def __init__(self, src, dst, here, there, where):
            self.src, self.dst, self.here, self.there, self.where = src, dst, here, there, where
            self.n = len(started)
            started.append(self)
            self.run(here, lambda copy: copy.start())

        def run(self, when, act):
            def go():
                act(
                    pltpu.make_async_remote_copy(
                        src_ref=self.src,
                        dst_ref=self.dst,
                        send_sem=send_sem.at[self.n],
                        recv_sem=recv_sem.at[self.n],
                        device_id=at(**self.where),
                        device_id_type=MESH,
                    )
                )

            if when is None:
                go()
            else:
                pl.when(when)(go)

        def wait_recv(self):
            self.run(self.there, lambda copy: copy.wait_recv())

        def wait_send(self):
            self.run(self.here, lambda copy: copy.wait_send())

    def send(src, dst, here=None, there=None, **where):
        return Copy(src, dst, here, there, where)

    edge, inner = (l == 0) | (l == 3), (l == 1) | (l == 2)

    class Gather:
        def __init__(self, axis, buf, first, second):
            self.axis, self.buf, self.first, self.second = axis, buf, first, second

        def start(self):
            self.right = send(self.buf(0), self.buf(3), **{self.axis: 1})
            self.left = send(self.buf(0), self.buf(1), **{self.axis: 3})

        def mid(self):
            self.right.wait_recv()
            self.far_right = send(self.first(self.buf(3)), self.first(self.buf(2)), **{self.axis: 1})
            self.left.wait_recv()
            self.far_left = send(self.second(self.buf(1)), self.second(self.buf(2)), **{self.axis: 3})

        def finish(self):
            self.far_right.wait_recv()
            self.far_left.wait_recv()

    class Scatter:
        def __init__(self, axis, part, wide, relay, full, first, second):
            self.axis, self.part, self.wide, self.relay, self.full = axis, part, wide, relay, full
            self.first, self.second = first, second

        def start(self):
            self.a = send(self.first(self.part(2)), self.relay(0), **{self.axis: 1})
            self.b = send(self.second(self.part(2)), self.relay(1), **{self.axis: 3})

        def mid(self):
            for copy, half, i in ((self.a, self.first, 1), (self.b, self.second, 3)):
                copy.wait_recv()
                lane = self.relay(i // 2)[...].astype(F32)
                half(self.part(i))[...] = (half(self.wide(i))[...] + lane).astype(BF)
            self.right = send(self.part(1), self.full(0), **{self.axis: 1})
            self.left = send(self.part(3), self.full(1), **{self.axis: 3})

        def finish(self):
            self.right.wait_recv()
            self.left.wait_recv()
            return (
                self.wide(0)[...]
                + self.full(0)[...].astype(F32)
                + self.full(1)[...].astype(F32)
            )

    class Direct:
        def __init__(self, axis, part, wide, full):
            self.axis, self.part, self.wide, self.full = axis, part, wide, full

        def start(self):
            self.copies = [
                send(self.part(i), self.full(i - 1), **{self.axis: i}) for i in (1, 3, 2)
            ]

        def finish(self):
            total = self.wide(0)[...]
            for i, copy in zip((1, 3, 2), self.copies):
                copy.wait_recv()
                total = total + self.full(i - 1)[...].astype(F32)
            return total

    class Reduce:
        def __init__(self, parts, core, sums, lands):
            self.parts, self.core, self.sums, self.lands = parts, core, sums, lands

        def start(self):
            self.pair = send(self.parts.at[1 - c], self.core, dc=1)

        def mid(self):
            self.pair.wait_recv()
            total = self.parts[c] + self.core[...]
            self.parts[c] = total
            self.sums[...] = total.astype(BF)
            self.hops = [
                send(self.sums.at[(l + i) % 4], self.lands.at[i - 1], dl=i) for i in (1, 2, 3)
            ]

        def finish(self):
            total = self.parts[c, l]
            for i, hop in enumerate(self.hops):
                hop.wait_recv()
                total = total + self.lands[i].astype(F32)
            return total.astype(BF)

    class AllReduce:
        def __init__(self, parts, core, sums, lands, out):
            self.parts, self.core, self.sums, self.lands, self.out = parts, core, sums, lands, out

        def start(self):
            self.pair = send(self.parts.at[1 - c], self.core, dc=1)

        def outer(self):
            self.pair.wait_recv()
            total = self.parts[c] + self.core[...]
            self.parts[c] = total

            @pl.when(edge)
            def _():
                self.sums[...] = total.astype(BF)

            self.up = send(self.sums, self.lands.at[0], edge, inner, dl=1 - 2 * (l % 2))

        def swap(self):
            self.up.wait_recv()

            @pl.when(inner)
            def _():
                total = self.parts[c] + self.lands[0].astype(F32)
                self.parts[c] = total
                self.sums[...] = total.astype(BF)

            self.over = send(self.sums, self.lands.at[1], inner, inner, dl=3 - 2 * l)

        def share(self):
            self.over.wait_recv()

            @pl.when(inner)
            def _():
                self.out[c] = (self.parts[c] + self.lands[1].astype(F32)).astype(BF)

            self.down = send(self.out.at[c], self.out.at[c], inner, edge, dl=1 - 2 * (l % 2))
            self.inner_pair = send(self.out.at[c], self.out.at[c], inner, inner, dc=1)

        def across(self):
            self.down.wait_recv()
            self.edge_pair = send(self.out.at[c], self.out.at[c], edge, edge, dc=1)

        def done(self):
            self.inner_pair.wait_recv()
            self.edge_pair.wait_recv()

    class Share:
        def __init__(self, out, task):
            self.out, self.task = out, task

        def start(self):
            self.out[c, l] = self.task.finish().astype(BF)
            own = self.out.at[c, l]
            self.up = send(own, own, edge, inner, dl=1 - 2 * (l % 2))

        def swap(self):
            self.up.wait_recv()
            pair = self.out.at[c, pl.ds(2 * (l // 2), 2)]
            self.over = send(pair, pair, inner, inner, dl=3 - 2 * l)

        def back(self):
            self.over.wait_recv()
            others = self.out.at[c, pl.ds(jnp.maximum(2 - l, 0) % 2, 3)]
            self.down = send(others, others, inner, edge, dl=1 - 2 * (l % 2))
            self.inner_pair = send(self.out.at[c], self.out.at[c], inner, inner, dc=1)

        def across(self):
            self.down.wait_recv()
            self.edge_pair = send(self.out.at[c], self.out.at[c], edge, edge, dc=1)

        def done(self):
            self.inner_pair.wait_recv()
            self.edge_pair.wait_recv()

    def rows(lo, hi):
        return lambda ref: ref.at[lo:hi]

    reads[7].wait()
    reads[8].wait()
    routes_t = routes[...].astype(F32)
    s.xb[0, 0, 0:FEAT] = tokens[...].T
    s.xb[0, 0, FEAT:XROWS] = jnp.concatenate(
        [routes_t, jnp.zeros((8, TOK), F32)], axis=0
    ).astype(BF)
    pl.semaphore_wait(barrier, len(peers))

    plan = Plan()

    upper = (iota((TOK, TOK), 0) < iota((TOK, TOK), 1)).astype(BF)

    def own_weights():
        for read in reads[0:4]:
            read.wait()

    def own_partials():
        reads[4].wait()
        reads[5].wait()
        for half, base in enumerate((gbase, ubase)):
            part = dot(tokens[...], base[...]).T
            for place in range(4):
                for core in range(2):
                    lo = (place * 2 + core) * HID
                    s.ap[core, place, half * HID : (half + 1) * HID] = part[lo : lo + HID]

    def own_slots():
        reads[6].wait()
        ranks = iota((64, TOK), 0)
        names = (
            ((x + ranks % 4) % 4) * 16 + ((y + (ranks // 4) % 4) % 4) * 4 + (h + ranks // 16) % 4
        ).astype(F32)
        chosen = [(names == routes_t[k : k + 1]).astype(F32) for k in range(8)]
        order = dot(sum(chosen).astype(BF), upper) + ranks.astype(F32) * CAP
        slot = [jnp.sum(chosen[k] * order, axis=0, keepdims=True) for k in range(8)]
        hid_t = jnp.concatenate([hidden[k] for k in range(8)], axis=1)
        for place in range(16):
            want = (iota((TOK, TOK), 0) + place * TOK).astype(F32)
            pick = jnp.concatenate([(slot[k] == want).astype(BF) for k in range(8)], axis=1)
            s.ho[place // 4, place % 4] = dot(hid_t, pick, 1, 1).astype(BF)
        s.hb[0, 0] = s.ho[0, 0]

    def tables():
        r4, c4 = iota((512, 512), 0), iota((512, 512), 1)
        s.pm[...] = (
            (r4 // 128 == (c4 // 32) % 4) & ((r4 // 32) % 4 == c4 // 128) & (r4 % 32 == c4 % 32)
        ).astype(BF)
        s.pb[...] = jnp.zeros_like(s.pb)

    def gather(name, task, link, size, after=()):
        plan.add(name + "0", task.start, after, 0.1, link, size)
        plan.add(name + "1", task.mid, [">" + name + "0"], 0.1, link, size / 2)
        plan.add(name + "2", task.finish, [">" + name + "1"], 0.05)

    def scatter(name, task, link, size, after, last, cost=0.3, late=()):
        plan.add(name + "0", task.start, after, 0.1, link, size / 2)
        plan.add(name + "1", task.mid, [">" + name + "0"] + list(after), 0.15, link, size)
        plan.add(name + "2", last, [">" + name + "1"] + list(late), cost)

    def direct(name, task, link, size, after, last, cost=0.2):
        plan.add(name + "0", task.start, after, 0.1, link, size)
        plan.add(name + "2", last, [">" + name + "0"], cost)

    x_halves = rows(0, 256), rows(256, XROWS)
    gather("xh", Gather("dh", lambda i: s.xb.at[i, 0], *x_halves), "z", 1.0)
    for q in (0, 1, 3, 2):
        task = Gather("dy", lambda i, q=q: s.xb.at[q, i], *x_halves)
        gather(f"xy{q}", task, "y", 0.25, [[], ["xh1"], ["xh2"], ["xh1"]][q])
    plan.add("wts", own_weights, [], 0.2)
    w_halves = rows(0, WROWS // 2), rows(WROWS // 2, WROWS)
    gather("wx", Gather("dx", lambda i: s.wb.at[i], *w_halves), "x", 0.6, ["wts"])

    def turn():
        for j in range(4):
            s.lt[j, 0:R] = s.wb[j, 0:512].T
            s.lt[j, R : 2 * R] = s.wb[j, 512:1024].T

    plan.add("lt", turn, ["wx2"], 0.5)

    act = Reduce(s.ap, s.ac, s.as_, s.az)

    def own_act():
        s.ab[0, 0] = act.finish()

    plan.add("actp", own_partials, [], 0.8)
    plan.add("act0", act.start, ["actp"], 0.1, "core", 0.375)
    plan.add("act1", act.mid, [">act0"], 0.3, "z", 0.375)
    plan.add("act2", own_act, [">act1"], 0.2)
    a_halves = rows(0, HID), rows(HID, 2 * HID)
    gather("ah", Gather("dh", lambda i: s.ab.at[i, 0], *a_halves), "z", 0.375, ["act2"])
    for q in (0, 1, 3, 2):
        task = Gather("dy", lambda i, q=q: s.ab.at[q, i], *a_halves)
        gather(f"ay{q}", task, "y", 0.1, [["act2"], ["ah1"], ["ah2"], ["ah1"]][q])

    hop = {}

    def hidden_near():
        hop["near"] = [send(s.ho.at[i], s.hm.at[4 - i], dh=i) for i in (1, 3)]

    def hidden_far():
        hop["far"] = [
            send(s.ho.at[2, 0:2], s.hw.at[0], dh=1),
            send(s.ho.at[2, 2:4], s.hw.at[1], dh=3),
        ]

    def hidden_on():
        hop["on"] = []
        for n, copy in enumerate(hop["far"]):
            copy.wait_recv()
            hop["on"].append(
                send(s.hw.at[n], s.hm.at[2, 2 * n : 2 * n + 2], dh=(1, 3)[n])
            )

    def hidden_pass(q):
        if q in (1, 3):
            hop["near"][{3: 0, 1: 1}[q]].wait_recv()
        elif q == 2:
            for copy in hop["on"]:
                copy.wait_recv()
        held = s.ho if q == 0 else s.hm
        if q:
            s.hb[q, 0] = s.hm[q, 0]
        hop[q] = [send(held.at[q, j], s.hb.at[q, 4 - j], dy=j) for j in (1, 2, 3)]

    plan.add("slots", own_slots, [], 1.5)
    plan.add("tab", tables, [], 0.4)
    plan.add("hn", hidden_near, ["slots", "xh1"], 0.1, "z", 0.75)
    plan.add("hf", hidden_far, ["slots", "xh1"], 0.1, "z", 0.375)
    plan.add("ho", hidden_on, [">hf"], 0.1, "z", 0.375)
    for q in range(4):
        from_ = [["slots"], [">hn"], [">ho"], [">hn"]][q]
        plan.add(f"hy{q}", lambda q=q: hidden_pass(q), from_, 0.1, "y", 0.15)

    experts = [(((x + j) % 4) * 16 + y * 4 + h).astype(F32) for j in range(4)]
    group_sum = (iota((16, TOK), 1) // 8 == iota((16, TOK), 0)).astype(BF)

    def select(q):
        named = []
        for b in range(4):
            block = s.xb[q, b, FEAT:XROWS].astype(F32)[0:8]
            named += [(block == experts[j]).astype(F32) for j in range(4)]
        hit = dot(group_sum, jnp.concatenate(named, axis=0).astype(BF))
        place = jnp.where(hit > 0.5, dot(hit.astype(BF), upper), -1.0)
        want = iota((CAP, TOK), 0).astype(F32)
        for b in range(4):
            for j in range(4):
                row = place[b * 4 + j : b * 4 + j + 1]
                s.pb[q, j * 128 + b * CAP : j * 128 + (b + 1) * CAP, b * TOK : (b + 1) * TOK] = (
                    row == want
                ).astype(BF)
        feats = jnp.concatenate([s.xb[q, b, 0:FEAT] for b in range(4)], axis=1)
        s.xs[q] = dot(feats, s.pb[q], 1, 1).astype(BF)

    def project(q):
        for j in range(4):
            value = dot(s.lt[j], s.xs[q, :, j * TOK : (j + 1) * TOK])
            s.lp[q, 0, j] = value[0:R]
            s.lp[q, 1, j] = value[R : 2 * R]

    def allreduce(name, task, after):
        plan.add(name + "0", task.start, after, 0.1, "core", 0.25)
        plan.add(name + "1", task.outer, [">" + name + "0"], 0.2, "zi", 0.25)
        plan.add(name + "2", task.swap, [">" + name + "1"], 0.2, "zm", 0.25)
        plan.add(name + "3", task.share, [">" + name + "2"], 0.2, "zo", 0.25)
        plan.add(name + "4", task.across, [">" + name + "3"], 0.1, "core", 0.125)
        plan.add(name + "5", task.done, [">" + name + "4"], 0.05)

    low = [
        AllReduce(s.lp.at[q], s.lc.at[q], s.ls.at[q], s.lz.at[q], s.lo.at[q])
        for q in range(4)
    ]
    dlow = [
        AllReduce(s.kp.at[q], s.kc.at[q], s.ks.at[q], s.kz.at[q], s.ko.at[q])
        for q in range(4)
    ]

    def middle(q):
        for copy in hop[q]:
            copy.wait_recv()
        acts = jnp.concatenate([s.ab[q, b] for b in range(4)], axis=1)
        acts = dot(acts, s.pb[q], 1, 1)
        cot = jnp.concatenate([s.hb[q, b] for b in range(4)], axis=1)
        cot = dot(cot, s.pm[...], 1, 1)
        gate = acts[0:HID] + jnp.concatenate(
            [dot(s.wb[j, 1024:1120], s.lo[q, 0, j]) for j in range(4)], axis=1
        )
        up = acts[HID : 2 * HID] + jnp.concatenate(
            [dot(s.wb[j, 1120:1216], s.lo[q, 1, j]) for j in range(4)], axis=1
        )
        sigma = jax.nn.sigmoid(gate)
        s.dg[q, 0:HID] = (cot * up * sigma * (1.0 + gate * (1.0 - sigma))).astype(BF)
        s.dg[q, HID : 2 * HID] = (cot * gate * sigma).astype(BF)
        for j in range(4):
            for half in range(2):
                s.kp[q, half, j] = dot(
                    s.wb[j, 1024 + half * HID : 1120 + half * HID],
                    s.dg[q, half * HID : (half + 1) * HID, j * TOK : (j + 1) * TOK],
                    0,
                    0,
                )

    def sums(q):
        part = dot(s.dg[q], s.pb[q])
        for b in range(4):
            s.gw[q, b] = part[:, b * TOK : (b + 1) * TOK]
            s.gp[q, b] = part[:, b * TOK : (b + 1) * TOK].astype(BF)

    def inputs(q, n):
        delta = []
        for j in range(4):
            lo = n * (FEAT // 2)
            left = jnp.concatenate(
                [s.wb[j, lo : lo + 256], s.wb[j, 512 + lo : 768 + lo]], axis=1
            )
            back = jnp.concatenate([s.ko[q, 0, j], s.ko[q, 1, j]], axis=0)
            delta.append(dot(left, back).astype(BF))
        part = dot(jnp.concatenate(delta, axis=1), s.pb[q])
        for b in range(4):
            s.dw[n, q, b] = part[:, b * TOK : (b + 1) * TOK]
            s.dp[n, q, b] = part[:, b * TOK : (b + 1) * TOK].astype(BF)

    def keep(task, wide, narrow):
        total = task.finish()
        wide[...] = total
        narrow[...] = total.astype(BF)

    def token_sums(q, half, first=0, last=4):
        return [
            s.gs[q, core, place, half * HID : (half + 1) * HID]
            for place in range(first, last)
            for core in range(2)
        ]

    def keep_inputs(q, n, task):
        lo = n * (FEAT // 2)
        total = task.finish()
        for half, base in enumerate((gbase, ubase)):
            total = total + dot(base[lo : lo + 256], jnp.concatenate(token_sums(q, half), axis=0))
        s.dv[n, q] = total
        s.dq[n, q] = total.astype(BF)

    d_halves = rows(0, 128), rows(128, 256)
    for q in (0, 1, 3, 2):
        plan.add(f"sel{q}", lambda q=q: select(q), ["tab", f"xy{q}2"], 0.5)
        plan.add(f"prj{q}", lambda q=q: project(q), ["lt", f"sel{q}"], 0.3)
        allreduce(f"lo{q}", low[q], [f"prj{q}"])
        plan.add(f"mid{q}", lambda q=q: middle(q), [f"lo{q}5", f"ay{q}2", f">hy{q}"], 0.5)
        allreduce(f"dl{q}", dlow[q], [f"mid{q}"])
        plan.add(f"sum{q}", lambda q=q: sums(q), [f"mid{q}"], 0.2)
        task = Direct(
            "dy",
            lambda i, q=q: s.gp.at[q, i],
            lambda i, q=q: s.gw.at[q, i],
            lambda i, q=q: s.gf.at[q, i],
        )
        share = Share(s.gs.at[q], task)
        plan.add(f"gy{q}0", task.start, [f"sum{q}"], 0.1, "y", 0.24)
        plan.add(f"ga{q}0", share.start, [f">gy{q}0"], 0.15, "zi", 0.095)
        plan.add(f"ga{q}1", share.swap, [f">ga{q}0"], 0.1, "zm", 0.19)
        plan.add(f"ga{q}2", share.back, [f">ga{q}1"], 0.1, "zo", 0.28)
        plan.add(f"ga{q}3", share.across, [f">ga{q}2"], 0.1, "core", 0.19)
        plan.add(f"ga{q}4", share.done, [f">ga{q}3"], 0.05)
        for n in range(2):
            plan.add(f"inp{q}{n}", lambda q=q, n=n: inputs(q, n), [f"dl{q}5"], 0.25)
            task = Scatter(
                "dy",
                lambda i, q=q, n=n: s.dp.at[n, q, i],
                lambda i, q=q, n=n: s.dw.at[n, q, i],
                lambda i, q=q, n=n: s.dr.at[n, q, i],
                lambda i, q=q, n=n: s.df.at[n, q, i],
                *d_halves,
            )
            scatter(
                f"d{n}y{q}", task, "y", 0.125, [f"inp{q}{n}"],
                lambda q=q, n=n, task=task: keep_inputs(q, n, task), 0.35, [f"ga{q}4"],
            )


    def ring_h(name, task, size, last, cost):
        along = name[:-1] + "y"
        near = [along + f"{q}2" for q in (1, 3)]
        plan.add(name + "0", task.start, [along + "22"], 0.1, "z", size / 2)
        plan.add(name + "1", task.mid, [">" + name + "0"] + near, cost, "z", size)
        plan.add(name + "2", last, [">" + name + "1", along + "02"], cost)

    def base_grads(n):
        whole = [
            jnp.concatenate(
                [
                    jnp.concatenate(token_sums(q, half, 2 * n, 2 * n + 2), axis=0)
                    for q in range(4)
                ],
                axis=1,
            )
            for half in range(2)
        ]
        for place in range(4):
            piece = jnp.concatenate(
                [s.xb[q, 0, place * 128 : (place + 1) * 128] for q in range(4)], axis=1
            )
            both = jnp.concatenate(
                [dot(piece, whole[half], 1, 1).reshape(16, 8, FF // 2) for half in range(2)],
                axis=1,
            ).reshape(4, 4, 16, FF // 2)
            if n == 0:
                s.bw[n, place] = both
                s.bg[n, place] = both.astype(BF)
            else:
                s.bw[n, :, place] = both
                s.bg[n, :, place] = both.astype(BF)

    def base_out(n, task):
        grad = task.finish()
        lo = n * (FF // 2)
        o_gb[:, lo : lo + FF // 2] = grad[0:8]
        o_ub[:, lo : lo + FF // 2] = grad[8:16]

    for n in range(2):
        plan.add(f"bas{n}", lambda n=n: base_grads(n), [f"ga{q}4" for q in range(4)], 0.7)
        bx = Scatter(
            ("dx", "dy")[n],
            lambda i, n=n: s.bg.at[n, ((x, y)[n] + i) % 4],
            lambda i, n=n: s.bw.at[n, ((x, y)[n] + i) % 4],
            lambda i, n=n: s.bxr.at[n, i],
            lambda i, n=n: s.bxf.at[n, i],
            rows(0, 2),
            rows(2, 4),
        )
        by = Direct(
            ("dy", "dx")[n],
            lambda i, n=n: s.by.at[n, ((y, x)[n] + i) % 4],
            lambda i, n=n: s.byw.at[n, ((y, x)[n] + i) % 4],
            lambda i, n=n: s.byf.at[n, i],
        )
        bz = Scatter(
            "dh",
            lambda i, n=n: s.bz.at[n, (h + i) % 4],
            lambda i, n=n: s.bzw.at[n, (h + i) % 4],
            lambda i, n=n: s.bzr.at[n, i, :, 0 : (256, 128)[i]],
            lambda i, n=n: s.bzf.at[n, i],
            lambda ref: ref.at[:, 0:256],
            lambda ref: ref.at[:, 256:384],
        )
        scatter(
            f"bx{n}", bx, ("x", "y")[n], 0.375, [f"bas{n}"],
            lambda n=n, bx=bx: keep(bx, s.byw.at[n], s.by.at[n]), 0.2,
        )
        direct(
            f"by{n}", by, ("y", "x")[n], 0.14, [f"bx{n}2"],
            lambda n=n, by=by: keep(by, s.bzw.at[n], s.bz.at[n]), 0.1,
        )
        scatter(f"bz{n}", bz, "z", 0.1, [f"by{n}2"], lambda n=n, bz=bz: base_out(n, bz), 0.1)

    def weight_grads():
        for j in range(4):
            slots = jnp.concatenate(
                [s.xs[q, :, j * TOK : (j + 1) * TOK] for q in range(4)], axis=1
            )
            for half in range(2):
                back = jnp.concatenate([s.ko[q, half, j] for q in range(4)], axis=1)
                left = dot(slots, back, 1, 1)
                s.ww[j, half * 512 : (half + 1) * 512] = left
                s.wg[j, half * 512 : (half + 1) * 512] = left.astype(BF)
                lows = jnp.concatenate([s.lo[q, half, j] for q in range(4)], axis=1)
                dgs = jnp.concatenate(
                    [
                        s.dg[q, half * HID : (half + 1) * HID, j * TOK : (j + 1) * TOK]
                        for q in range(4)
                    ],
                    axis=1,
                )
                right = dot(dgs, lows, 1, 1)
                s.ww[j, 1024 + half * HID : 1120 + half * HID] = right
                s.wg[j, 1024 + half * HID : 1120 + half * HID] = right.astype(BF)

    wgx = Scatter(
        "dx",
        lambda i: s.wg.at[i],
        lambda i: s.ww.at[i],
        lambda i: s.wr.at[i],
        lambda i: s.wf.at[i],
        *w_halves,
    )

    def weight_out():
        grads = wgx.finish()
        o_gl[0] = grads[0:512]
        o_ul[0] = grads[512:1024]
        o_gr[0] = grads[1024:1120]
        o_ur[0] = grads[1120:1216]

    plan.add("wgr", weight_grads, [f"dl{q}5" for q in range(4)], 0.8)
    scatter("wgx", wgx, "x", 0.6, ["wgr"], weight_out, 0.3)

    dh = [
        Scatter(
            "dh",
            lambda i, n=n: s.dq.at[n, i],
            lambda i, n=n: s.dv.at[n, i],
            lambda i, n=n: s.er.at[n, i],
            lambda i, n=n: s.ef.at[n, i],
            *d_halves,
        )
        for n in range(2)
    ]

    def token_out(n):
        lo = n * (FEAT // 2)
        o_tok[:, lo : lo + 256] = dh[n].finish().T.astype(BF)

    for n in range(2):
        ring_h(f"d{n}h", dh[n], 0.5, lambda: None, 0.2)
        plan.add(f"tok{n}", lambda n=n: token_out(n), [f"d{n}h2"], 0.2)

    for name in plan.order():
        plan.steps[name][0]()
    for copy in started:
        copy.wait_send()


def hand_on(*refs):
    for given, taken in zip(refs[:7], refs[7:]):
        taken[...] = given[...]


def local(tokens, routes, hidden, gbase, ubase, gleft, uleft, gright, uright):
    vmem = pl.BlockSpec(memory_space=pltpu.VMEM)
    anywhere = pl.BlockSpec(memory_space=pl.ANY)
    shapes = [
        ((TOK, FEAT), BF),
        ((8, FF), F32),
        ((8, FF), F32),
        ((1, FEAT, R), F32),
        ((1, FEAT, R), F32),
        ((1, HID, R), F32),
        ((1, HID, R), F32),
    ]
    outs = pl.pallas_call(
        kernel,
        out_shape=[jax.ShapeDtypeStruct(*shape) for shape in shapes],
        in_specs=[anywhere] * 9,
        out_specs=[vmem] * 7,
        scratch_shapes=[pltpu.VMEM(*shape) for shape in SCRATCH.values()]
        + [pltpu.SemaphoreType.DMA((SEMS,)), pltpu.SemaphoreType.DMA((SEMS,)), pltpu.SemaphoreType.DMA((9,))],
        compiler_params=pltpu.CompilerParams(
            collective_id=0, has_side_effects=True, vmem_limit_bytes=60 * 1024 * 1024
        ),
    )(
        tokens,
        routes.T,
        jnp.transpose(hidden, (1, 2, 0)),
        gbase,
        ubase,
        gleft,
        uleft,
        jnp.swapaxes(gright, 1, 2),
        jnp.swapaxes(uright, 1, 2),
    )
    outs = pl.pallas_call(
        hand_on,
        out_shape=[jax.ShapeDtypeStruct(*shape) for shape in shapes],
        in_specs=[vmem] * 7,
        out_specs=[vmem] * 7,
    )(*outs)
    return (*outs[:5], jnp.swapaxes(outs[5], 1, 2), jnp.swapaxes(outs[6], 1, 2))


def solution(mesh):
    return jax.shard_map(
        local,
        mesh=mesh,
        in_specs=(
            P("expert", "fsdp"),
            P("expert", None),
            P("expert", None, "fsdp"),
            P("fsdp", None),
            P("fsdp", None),
            P("expert", "fsdp", None),
            P("expert", "fsdp", None),
            P("expert", None, "fsdp"),
            P("expert", None, "fsdp"),
        ),
        out_specs=(
            P("expert", "fsdp"),
            P(("fsdp", "expert"), None),
            P(("fsdp", "expert"), None),
            P("expert", "fsdp", None),
            P("expert", "fsdp", None),
            P("expert", None, "fsdp"),
            P("expert", None, "fsdp"),
        ),
        check_vma=False,
    )
```
